512 devices in a mesh: row: 16 (over y_hi, x, core), col: 32 (over z, y_lo).
Axes of the slice: x: 4, y: 4 (y_hi: 2, y_lo: 2; y = y_hi * 2 + y_lo), z: 16, core: 2. Of those that a mesh axis runs over, the one named last changes fastest.
Arguments:
- section_a: bfloat16 [256, 1024, 256], P('row', 'col'), may hold values from -16 to 16
- section_b: bfloat16 [256, 1024, 256], P('row', 'col'), may hold values from -16 to 16
- ln_gain: float32 [256], replicated, may hold values from 0.5 to 1.5
- ln_shift: float32 [256], replicated, may hold values from -3 to 3
- w_qkv: bfloat16 [256, 768], replicated, may hold values from -0.375 to 0.375
- b_qkv: float32 [768], replicated, may hold values from -3 to 3
- rel_table: float32 [8, 225], replicated, may hold values from -4 to 4
- w_out: bfloat16 [256, 256], replicated, may hold values from -0.375 to 0.375
- b_out: float32 [256], replicated, may hold values from -3 to 3
- w_hid: bfloat16 [289, 256], replicated, may hold values from -0.375 to 0.375
- b_hid: float32 [256], replicated, may hold values from -3 to 3
- w_flow: bfloat16 [256, 2], replicated, may hold values from -0.375 to 0.375
- b_flow: float32 [2], replicated, may hold values from -3 to 3
Outputs:
- flow: float32 [2, 256, 1024], P(None, 'row', 'col')
The draws below stay inside these ranges and needn't reach their ends.
All inputs are finite; a program needn't handle non-finite values.
Results may differ from the reference program's by a relative error of at most 0.04.
Values may be sent and summed in bfloat16 or wider, within the bound.
No kernel may reach another device: no remote copies, remote signals or barrier semaphores. Data moves between devices by JAX's collectives and lax.ppermute only.
A program may use at most 64 MiB of HBM per device.

```python
import jax
import jax.numpy as jnp
import numpy as np
from jax import lax

C = 256
HEADS = 8
HEAD = 32
WIN = 8
SHIFT = 4
RADIUS = 8
OFFS = 289
HID = 256
NR = 256
NC = 1024


def shared_sections(key):
    keys = jax.random.split(key, 3)
    base = jnp.clip(jax.random.normal(keys[0], (NR, NC, C), jnp.float32), -4.5, 4.5)
    noise = jnp.clip(jax.random.normal(keys[2], (NR, NC, C), jnp.float32), -4.5, 4.5)
    patch_rows = (NR + 23) // 24
    patch_cols = (NC + 39) // 40
    moves = jax.random.randint(keys[1], (2, patch_rows, patch_cols), -RADIUS, RADIUS + 1)
    row_places = jnp.arange(NR, dtype=jnp.int32)
    col_places = jnp.arange(NC, dtype=jnp.int32)
    row_patch = row_places // 24
    col_patch = col_places // 40
    move_rows = moves[0][row_patch[:, None], col_patch[None, :]]
    move_cols = moves[1][row_patch[:, None], col_patch[None, :]]
    source_rows = (row_places[:, None] - move_rows) % NR
    source_cols = (col_places[None, :] - move_cols) % NC
    moved = base[source_rows, source_cols]
    return (base, 0.25 * moved + 0.9 * noise)


def draw_section_a(key, part):
    return shared_sections(key)[0].astype(jnp.bfloat16)


def draw_section_b(key, part):
    return shared_sections(key)[1].astype(jnp.bfloat16)


def scatter_about(key, dims, scale, most, kind=jnp.bfloat16):
    drawn = jax.random.normal(key, dims, jnp.float32) * scale
    return jnp.minimum(jnp.maximum(drawn, -most), most).astype(kind)


def setup_inputs(seed: int = 0) -> dict:
    streams_of = jax.random.split(jax.random.key(seed), 14)
    section_a = draw_section_a(jax.random.fold_in(streams_of[13], 71), 0)
    section_b = draw_section_b(jax.random.fold_in(streams_of[13], 71), 0)
    ln_gain = jnp.clip(1.0 + 0.1 * jax.random.normal(streams_of[2], (C,), jnp.float32), 0.5, 1.5)
    ln_shift = scatter_about(streams_of[3], (C,), 0.5, 3.0, jnp.float32)
    w_qkv = scatter_about(streams_of[4], (C, 3 * C), C ** -0.5, 0.375)
    b_qkv = scatter_about(streams_of[5], (3 * C,), 0.5, 3.0, jnp.float32)
    rel_table = scatter_about(streams_of[6], (HEADS, (2 * WIN - 1) * (2 * WIN - 1)), 1.0, 4.0, jnp.float32)
    w_out = scatter_about(streams_of[7], (C, C), C ** -0.5, 0.375)
    b_out = scatter_about(streams_of[8], (C,), 0.5, 3.0, jnp.float32)
    w_hid = scatter_about(streams_of[9], (OFFS, HID), OFFS ** -0.5, 0.375)
    b_hid = scatter_about(streams_of[10], (HID,), 0.5, 3.0, jnp.float32)
    w_flow = scatter_about(streams_of[11], (HID, 2), HID ** -0.5, 0.375)
    b_flow = scatter_about(streams_of[12], (2,), 0.5, 3.0, jnp.float32)
    return {"section_a": section_a, "section_b": section_b, "ln_gain": ln_gain, "ln_shift": ln_shift, "w_qkv": w_qkv, "b_qkv": b_qkv, "rel_table": rel_table, "w_out": w_out, "b_out": b_out, "w_hid": w_hid, "b_hid": b_hid, "w_flow": w_flow, "b_flow": b_flow}


def relative_index():
    places = np.arange(WIN)
    grid_rows, grid_cols = np.meshgrid(places, places, indexing='ij')
    flat_rows = grid_rows.reshape(-1)
    flat_cols = grid_cols.reshape(-1)
    rel_rows = flat_rows[:, None] - flat_rows[None, :] + WIN - 1
    rel_cols = flat_cols[:, None] - flat_cols[None, :] + WIN - 1
    return rel_rows * (2 * WIN - 1) + rel_cols

def layer_norm(features, ln_gain, ln_shift):
    values = features.astype(jnp.float32)
    average = lax.optimization_barrier(jnp.mean(values, axis=-1, keepdims=True))
    centred = values - average
    variance = lax.optimization_barrier(jnp.mean(centred * centred, axis=-1, keepdims=True))
    return (centred * lax.rsqrt(variance + 1e-05) * ln_gain + ln_shift).astype(jnp.bfloat16)

def labels_of(row_places, col_places, total_rows, total_cols):
    row_label = (row_places >= total_rows - WIN).astype(jnp.int32) + (row_places >= total_rows - SHIFT).astype(jnp.int32)
    col_label = (col_places >= total_cols - WIN).astype(jnp.int32) + (col_places >= total_cols - SHIFT).astype(jnp.int32)
    return row_label[:, None] * 3 + col_label[None, :]

def attend(rolled, labels, w_qkv, b_qkv, position_bias, w_out, b_out):
    height, width = (rolled.shape[0], rolled.shape[1])
    high, wide = (height // WIN, width // WIN)
    windows = rolled.reshape(high, WIN, wide, WIN, C).transpose(0, 2, 1, 3, 4).reshape(-1, C)
    win_labels = labels.reshape(high, WIN, wide, WIN).transpose(0, 2, 1, 3).reshape(high * wide, WIN * WIN)
    qkv = (jnp.dot(windows, w_qkv, preferred_element_type=jnp.float32) + b_qkv).astype(jnp.bfloat16)
    qkv = qkv.reshape(high * wide, WIN * WIN, 3, HEADS, HEAD)
    queries = qkv[:, :, 0].astype(jnp.float32)
    key_part = qkv[:, :, 1].astype(jnp.float32)
    values = qkv[:, :, 2].astype(jnp.float32)
    masking = jnp.where(win_labels[:, :, None] == win_labels[:, None, :], 0.0, -100.0).astype(jnp.float32)
    scores = jnp.einsum('gqhd,gkhd->ghqk', queries, key_part) * HEAD ** (-0.5)
    scores = scores + position_bias[None] + masking[:, None]
    weights = jax.nn.softmax(scores, axis=-1).astype(jnp.bfloat16)
    mixed = jnp.einsum('ghqk,gkhd->gqhd', weights.astype(jnp.float32), values).astype(jnp.bfloat16)
    mixed = mixed.reshape(-1, C)
    attended = (jnp.dot(mixed, w_out, preferred_element_type=jnp.float32) + b_out).astype(jnp.bfloat16)
    return attended.reshape(high, wide, WIN, WIN, C).transpose(0, 2, 1, 3, 4).reshape(height, width, C)

def flow_head(corr, w_hid, b_hid, w_flow, b_flow):
    probability = jax.nn.softmax(corr, axis=-1)
    offsets = jnp.arange(OFFS, dtype=jnp.int32)
    disp_rows = (offsets // (2 * RADIUS + 1) - RADIUS).astype(jnp.float32)
    disp_cols = (offsets % (2 * RADIUS + 1) - RADIUS).astype(jnp.float32)
    expected = jnp.stack([lax.optimization_barrier(jnp.sum(probability * disp_rows, axis=-1)), lax.optimization_barrier(jnp.sum(probability * disp_cols, axis=-1))], axis=-1)
    scaled = (probability * OFFS).astype(jnp.bfloat16)
    lead = scaled.shape[:-1]
    hidden = jax.nn.gelu(jnp.dot(scaled.reshape(-1, OFFS), w_hid, preferred_element_type=jnp.float32) + b_hid).astype(jnp.bfloat16)
    regressed = jnp.dot(hidden, w_flow, preferred_element_type=jnp.float32) + b_flow
    return expected + regressed.reshape(lead + (2,))

def block(section, ln_gain, ln_shift, w_qkv, b_qkv, position_bias, w_out, b_out):
    rolled = jnp.roll(section, (-SHIFT, -SHIFT), (0, 1))

    def one_band(band_index):
        piece = lax.dynamic_slice_in_dim(rolled, band_index * WIN, WIN, 0)
        normed = layer_norm(piece, ln_gain, ln_shift)
        row_places = band_index * WIN + jnp.arange(WIN, dtype=jnp.int32)
        labels = labels_of(row_places, jnp.arange(NC, dtype=jnp.int32), NR, NC)
        return attend(normed, labels, w_qkv, b_qkv, position_bias, w_out, b_out)
    attended = lax.map(one_band, jnp.arange(NR // WIN, dtype=jnp.int32)).reshape(NR, NC, C)
    attended = jnp.roll(attended, (SHIFT, SHIFT), (0, 1))
    return (section.astype(jnp.float32) + attended.astype(jnp.float32)).astype(jnp.bfloat16)

def reference(section_a, section_b, ln_gain, ln_shift, w_qkv, b_qkv, rel_table, w_out, b_out, w_hid, b_hid, w_flow, b_flow):
    position_bias = rel_table[:, relative_index()]
    feature_a = block(section_a, ln_gain, ln_shift, w_qkv, b_qkv, position_bias, w_out, b_out)
    feature_b = block(section_b, ln_gain, ln_shift, w_qkv, b_qkv, position_bias, w_out, b_out)
    padded = jnp.pad(feature_b, ((RADIUS, RADIUS), (RADIUS, RADIUS), (0, 0)))

    def one_band(band_index):
        piece = lax.dynamic_slice_in_dim(feature_a, band_index * WIN, WIN, 0).astype(jnp.float32)
        columns = []
        for row_off in range(2 * RADIUS + 1):
            reach = lax.dynamic_slice_in_dim(padded, band_index * WIN + row_off, WIN, 0)
            stacked = jnp.stack([reach[:, col_off:col_off + NC] for col_off in range(2 * RADIUS + 1)], axis=2)
            columns.append(jnp.einsum('yxc,yxdc->yxd', piece, stacked.astype(jnp.float32)))
        corr = jnp.concatenate(columns, axis=-1) * C ** (-0.5)
        return flow_head(corr, w_hid, b_hid, w_flow, b_flow)
    flows = lax.map(one_band, jnp.arange(NR // WIN, dtype=jnp.int32)).reshape(NR, NC, 2)
    return jnp.transpose(flows, (2, 0, 1))
```

```python
import jax
import jax.numpy as jnp
import numpy as np
from jax import lax
from jax.experimental import pallas as pl
from jax.experimental.pallas import tpu as pltpu
from jax.sharding import PartitionSpec as P

C = 256
HEADS = 8
HEAD = 32
WIN = 8
SHIFT = 4
RADIUS = 8
SPAN = 2 * RADIUS + 1
OFFS = SPAN * SPAN
ROWS = 16
COLS = 32
HALO_A = 4
HALO_B = 12
HIGH_A, WIDE_A = 3, 5
HIGH_B, WIDE_B = 5, 7
CELLS = WIN * WIN
COUNT_A = HIGH_A * WIDE_A
COUNT_B = HIGH_B * WIDE_B
BLOCK = HIGH_B * CELLS
BLOCKS = (COUNT_A + COUNT_B) // HIGH_B
KEYS = 64
REACH = 18 * KEYS
LOG2E = 1.4426950408889634
NT = (((1,), (1,)), ((), ()))


def ring(array, axis, by):
    peers = lax.axis_size(axis)
    return lax.ppermute(array, axis, [(i, (i + by) % peers) for i in range(peers)])


def dot(left, right):
    return jnp.dot(left, right, preferred_element_type=jnp.float32)


def body(
    marks,
    xb,
    xa,
    gain,
    shift,
    w_qkv,
    b_qkv,
    bias,
    w_out,
    b_out,
    w_even,
    w_odd,
    w_off,
    b_hid,
    w_flow,
    b_flow,
    mirror,
    unmirror,
    out,
    q_s,
    k_s,
    v_s,
    mix_s,
    fb,
    fa,
    e_s,
):
    def project(x, row):
        x = x.astype(jnp.float32)
        centred = x - jnp.mean(x, axis=-1, keepdims=True)
        variance = jnp.mean(centred * centred, axis=-1, keepdims=True)
        normed = centred * lax.rsqrt(variance + 1e-05) * gain[...] + shift[...]
        qkv = dot(normed.astype(jnp.bfloat16), w_qkv[...]) + b_qkv[...]
        rows = pl.ds(row, BLOCK)
        q_s[rows] = (qkv[:, :C] * (HEAD**-0.5 * LOG2E)).astype(jnp.bfloat16)
        k_s[rows] = qkv[:, C : 2 * C].astype(jnp.bfloat16)
        v_s[rows] = qkv[:, 2 * C :].astype(jnp.bfloat16)

    @pl.loop(0, WIDE_B)
    def _(j):
        row = pl.multiple_of(j * BLOCK, BLOCK)
        project(xb[pl.ds(row, BLOCK)], row)

    @pl.loop(0, BLOCKS - WIDE_B)
    def _(j):
        row = pl.multiple_of(j * BLOCK, BLOCK)
        project(xa[pl.ds(row, BLOCK)], pl.multiple_of(row + WIDE_B * BLOCK, BLOCK))

    lanes = lax.broadcasted_iota(jnp.int32, (1, C), 1) // HEAD
    picks = [(lanes == h).astype(jnp.float32).astype(jnp.bfloat16) for h in range(HEADS)]
    ones = jnp.concatenate(
        [jnp.broadcast_to(p, (CELLS, C)) for p in picks], axis=0
    )
    half = lax.broadcasted_iota(jnp.int32, (CELLS, 128), 1) < CELLS

    def attend(window):
        rows = pl.ds(pl.multiple_of(window * CELLS, CELLS), CELLS)
        q, k, v = q_s[rows], k_s[rows], v_s[rows]
        keys = jnp.concatenate([k * p for p in picks], axis=0)
        values = jnp.concatenate([v * p for p in picks], axis=0)
        scores = lax.dot_general(q, keys, NT, preferred_element_type=jnp.float32)
        scores = scores + bias[marks[window]]
        weights = []
        for pair in range(HEADS // 2):
            s = scores[:, 128 * pair : 128 * (pair + 1)]
            low = jnp.max(jnp.where(half, s, -jnp.inf), axis=-1, keepdims=True)
            top = jnp.max(jnp.where(half, -jnp.inf, s), axis=-1, keepdims=True)
            weights.append(jnp.exp2(s - jnp.where(half, low, top)).astype(jnp.bfloat16))
        weights = jnp.concatenate(weights, axis=1)
        mix_s[rows] = (dot(weights, values) / dot(weights, ones)).astype(jnp.bfloat16)

    @pl.loop(0, BLOCKS)
    def _(block):
        for i in range(HIGH_B):
            attend(block * HIGH_B + i)

    row_start = marks[64] * ROWS
    col_start = marks[65] * COLS
    total_rows = marks[66] * ROWS
    total_cols = marks[67] * COLS

    def features(x, mixed):
        attended = (dot(mixed, w_out[...]) + b_out[...]).astype(jnp.bfloat16)
        return x.astype(jnp.float32) + attended.astype(jnp.float32)

    col_places = col_start - HALO_B + lax.broadcasted_iota(jnp.int32, (KEYS, 1), 0)
    col_inside = (col_places >= 0) & (col_places < total_cols)
    blank = jnp.zeros((KEYS - WIDE_B * WIN, C), jnp.float32)

    @pl.loop(0, HIGH_B)
    def _(i):
        starts = [
            pl.multiple_of(j * BLOCK + i * CELLS, CELLS) for j in range(WIDE_B)
        ]
        x = jnp.concatenate([xb[pl.ds(s, CELLS)] for s in starts], axis=0)
        mixed = jnp.concatenate([mix_s[pl.ds(s, CELLS)] for s in starts], axis=0)
        f = features(x, mixed)
        for r in range(WIN):
            row = jnp.concatenate(
                [f[CELLS * j + WIN * r : CELLS * j + WIN * (r + 1)] for j in range(WIDE_B)]
                + [blank],
                axis=0,
            )
            place = row_start - HALO_B + i * WIN + r
            inside = col_inside & (place >= 0) & (place < total_rows)
            fb[i * WIN + r] = jnp.where(inside, row, 0.0).astype(jnp.bfloat16)

    @pl.loop(0, HIGH_A)
    def _(i):
        starts = [
            pl.multiple_of(j * HIGH_A * CELLS + i * CELLS, CELLS) for j in range(WIDE_A)
        ]
        x = jnp.concatenate([xa[pl.ds(s, CELLS)] for s in starts], axis=0)
        mixed = jnp.concatenate(
            [mix_s[pl.ds(pl.multiple_of(s + WIDE_B * BLOCK, CELLS), CELLS)] for s in starts],
            axis=0,
        )
        f = features(x, mixed)
        f = dot(mirror[...], f.astype(jnp.bfloat16)).astype(jnp.bfloat16)
        fa[pl.ds(i * WIN, WIN)] = f.reshape(WIN, COLS, C)

    lane = lax.broadcasted_iota(jnp.int32, (COLS, 128), 1)
    near = lane % KEYS < SPAN
    first = near & (lane < KEYS)
    second = near & (lane >= KEYS)

    @pl.loop(0, ROWS // 4)
    def _(t):
        queries = fa[pl.ds(HALO_A + 4 * t, 4)].reshape(4 * COLS, C)
        keys = fb[pl.ds(HALO_B - RADIUS + 4 * t, 20)].reshape(20 * KEYS, C)
        gram = lax.dot_general(queries, keys, NT, preferred_element_type=jnp.float32)
        for r in range(4):
            tiles = []
            for n in range(9):
                at = 128 * (n + r // 2)
                tile = gram[COLS * r : COLS * (r + 1), at : at + 128]
                tile = pltpu.roll(tile, 128 - HALO_A - COLS + 1, 1, stride=1, stride_axis=0)
                keep = near
                if r % 2 == 0 and n == 8:
                    keep = first
                if r % 2 == 1 and n == 0:
                    keep = second
                tiles.append(jnp.where(keep, tile * (C**-0.5 * LOG2E), -1e30))
            most = tiles[0]
            for tile in tiles[1:]:
                most = jnp.maximum(most, tile)
            most = jnp.max(most, axis=-1, keepdims=True)
            rows = pl.ds(pl.multiple_of((2 * t + r // 2) * COLS, COLS), COLS)
            for n in range(9):
                e_s[r % 2, rows, 128 * n : 128 * (n + 1)] = jnp.exp2(tiles[n] - most).astype(
                    jnp.bfloat16
                )

    for par, w_hid in enumerate((w_even, w_odd)):
        e = e_s[par]
        sums = dot(e, w_off[par])
        scale = 1.0 / sums[:, 2:3]
        hidden = jax.nn.gelu(dot(e, w_hid[...]) * (scale * OFFS) + b_hid[...])
        flow = sums * scale + dot(hidden.astype(jnp.bfloat16), w_flow[...]) + b_flow[...]
        flow = jnp.dot(
            unmirror[...],
            flow,
            precision=lax.Precision.HIGHEST,
            preferred_element_type=jnp.float32,
        ).T
        for t in range(ROWS // 2):
            out[:, 2 * t + par, :] = flow[0:2, COLS * t : COLS * (t + 1)]


def skewed(w_hid):
    w = w_hid.reshape(SPAN, SPAN, C)
    w = jnp.pad(w, ((0, 0), (0, KEYS - SPAN), (0, 0)))
    even = jnp.pad(w, ((0, 1), (0, 0), (0, 0))).reshape(REACH, C)
    odd = jnp.pad(w, ((1, 0), (0, 0), (0, 0))).reshape(REACH, C)
    return even, odd


def offsets():
    table = np.zeros((2, 18, KEYS, 128), np.float32)
    for par in range(2):
        for dr in range(SPAN):
            for dc in range(SPAN):
                table[par, dr + par, dc, :3] = (dr - RADIUS, dc - RADIUS, 1.0)
    return jnp.asarray(table.reshape(2, REACH, 128), jnp.bfloat16)


def mirrors():
    turn = np.zeros((WIN, COLS, WIDE_A, WIN, WIN), np.float32)
    for r in range(WIN):
        for c in range(COLS):
            place = HALO_A + COLS - 1 - c
            turn[r, c, place // WIN, r, place % WIN] = 1.0
    turn = jnp.asarray(turn.reshape(WIN * COLS, WIDE_A * CELLS), jnp.bfloat16)
    back = np.kron(np.eye(ROWS // 2, dtype=np.float32), np.eye(COLS, dtype=np.float32)[::-1])
    return turn, jnp.asarray(back)


def position_bias(rel_table):
    places = np.arange(CELLS)
    rows, cols = places // WIN, places % WIN
    index = (rows[:, None] - rows[None, :] + WIN - 1) * (2 * WIN - 1) + (
        cols[:, None] - cols[None, :] + WIN - 1
    )
    pick = np.zeros(((2 * WIN - 1) ** 2, CELLS * CELLS), np.float32)
    pick[index.reshape(-1), np.arange(CELLS * CELLS)] = 1.0
    pick = jnp.asarray(pick, jnp.bfloat16)
    high = rel_table.astype(jnp.bfloat16)
    rest = rel_table - high.astype(jnp.float32)
    mid = rest.astype(jnp.bfloat16)
    low = (rest - mid.astype(jnp.float32)).astype(jnp.bfloat16)
    table = jnp.sum(
        dot(jnp.concatenate([high, mid, low], axis=0), pick).reshape(3, HEADS, CELLS, CELLS),
        axis=0,
    )
    split_r = (rows[:, None] < SHIFT) != (rows[None, :] < SHIFT)
    split_c = (cols[:, None] < SHIFT) != (cols[None, :] < SHIFT)
    masks = np.stack([split_r & False, split_r, split_c, split_r | split_c])
    masks = jnp.asarray(np.where(masks, -100.0, 0.0), jnp.float32)
    full = (table.transpose(1, 0, 2)[None] + masks[:, :, None, :]) * LOG2E
    return full.reshape(4, CELLS, HEADS * CELLS)


def window_marks(row, col, rows, cols):
    def marks(high, wide, inset):
        i = jnp.arange(high, dtype=jnp.int32)[None, :]
        j = jnp.arange(wide, dtype=jnp.int32)[:, None]
        on_row = ((row == 0) & (i == inset)) | ((row == rows - 1) & (i == high - 1 - inset))
        on_col = ((col == 0) & (j == inset)) | ((col == cols - 1) & (j == wide - 1 - inset))
        return (on_row.astype(jnp.int32) + 2 * on_col.astype(jnp.int32)).reshape(-1)

    return jnp.concatenate(
        [
            marks(HIGH_B, WIDE_B, 1),
            marks(HIGH_A, WIDE_A, 0),
            jnp.zeros((14,), jnp.int32),
            jnp.stack([row, col, jnp.int32(rows), jnp.int32(cols)]),
        ]
    )


def split_cols(cells, wide):
    return cells.reshape(cells.shape[0], wide, WIN, C).transpose(1, 0, 2, 3)


def shards(
    section_a,
    section_b,
    ln_gain,
    ln_shift,
    w_qkv,
    b_qkv,
    rel_table,
    w_out,
    b_out,
    w_hid,
    b_hid,
    w_flow,
    b_flow,
):
    rows, cols = lax.axis_size("row"), lax.axis_size("col")
    row, col = lax.axis_index("row"), lax.axis_index("col")

    left = jnp.concatenate([section_b[:, :HALO_B], section_a[:, :HALO_A]], axis=1)
    right = jnp.concatenate([section_b[:, -HALO_B:], section_a[:, -HALO_A:]], axis=1)
    after = ring(left, "col", -1)
    before = ring(right, "col", 1)
    wide_b = jnp.concatenate([before[:, :HALO_B], section_b, after[:, :HALO_B]], axis=1)
    wide_a = jnp.concatenate([before[:, HALO_B:], section_a, after[:, HALO_B:]], axis=1)
    wide_b = split_cols(wide_b, WIDE_B)
    wide_a = split_cols(wide_a, WIDE_A)

    def pack(b_part, a_part):
        return jnp.concatenate([b_part.reshape(-1, C), a_part.reshape(-1, C)], axis=0)

    def unpack(flat):
        cut = WIDE_B * HALO_B * WIN
        return (
            flat[:cut].reshape(WIDE_B, HALO_B, WIN, C),
            flat[cut:].reshape(WIDE_A, HALO_A, WIN, C),
        )

    below_b, below_a = unpack(ring(pack(wide_b[:, :HALO_B], wide_a[:, :HALO_A]), "row", -1))
    above_b, above_a = unpack(ring(pack(wide_b[:, -HALO_B:], wide_a[:, -HALO_A:]), "row", 1))
    xb = jnp.concatenate([above_b, wide_b, below_b], axis=1).reshape(-1, C)
    xa = jnp.concatenate([above_a, wide_a, below_a], axis=1).reshape(-1, C)

    w_even, w_odd = skewed(w_hid)
    flow_pad = jnp.pad(w_flow, ((0, 0), (0, 126)))
    b_flow_pad = jnp.pad(b_flow, (0, 126))
    total = (COUNT_A + COUNT_B) * CELLS
    whole = pl.BlockSpec(memory_space=pltpu.VMEM)
    call = pl.pallas_call(
        body,
        out_shape=jax.ShapeDtypeStruct((2, ROWS, COLS), jnp.float32),
        in_specs=[pl.BlockSpec(memory_space=pltpu.SMEM)] + [whole] * 17,
        out_specs=whole,
        scratch_shapes=[
            pltpu.VMEM((total, C), jnp.bfloat16),
            pltpu.VMEM((total, C), jnp.bfloat16),
            pltpu.VMEM((total, C), jnp.bfloat16),
            pltpu.VMEM((total, C), jnp.bfloat16),
            pltpu.VMEM((HIGH_B * WIN, KEYS, C), jnp.bfloat16),
            pltpu.VMEM((HIGH_A * WIN, COLS, C), jnp.bfloat16),
            pltpu.VMEM((2, ROWS // 2 * COLS, REACH), jnp.bfloat16),
        ],
        compiler_params=pltpu.CompilerParams(vmem_limit_bytes=40 * 1024 * 1024),
    )
    return call(
        window_marks(row, col, rows, cols),
        xb,
        xa,
        ln_gain[None],
        ln_shift[None],
        w_qkv,
        b_qkv[None],
        position_bias(rel_table),
        w_out,
        b_out[None],
        w_even,
        w_odd,
        offsets(),
        b_hid[None],
        flow_pad,
        b_flow_pad[None],
        *mirrors(),
    )


def solution(mesh):
    placed = (P("row", "col", None),) * 2 + (P(),) * 11
    return jax.shard_map(
        shards, mesh=mesh, in_specs=placed, out_specs=P(None, "row", "col"), check_vma=False
    )
```

```python
import jax
import jax.numpy as jnp
import numpy as np
from jax import lax
from jax.experimental import pallas as pl
from jax.experimental.pallas import tpu as pltpu
from jax.sharding import PartitionSpec as P

C = 256
HEADS = 8
HEAD = 32
WIN = 8
SHIFT = 4
RADIUS = 8
SPAN = 2 * RADIUS + 1
OFFS = SPAN * SPAN
ROWS = 16
COLS = 32
HALO_A = 4
HALO_B = 12
HIGH_A, WIDE_A = 3, 5
HIGH_B, WIDE_B = 5, 7
CELLS = WIN * WIN
COUNT_A = HIGH_A * WIDE_A
COUNT_B = HIGH_B * WIDE_B
BLOCK = 640
TOTAL = (COUNT_A + COUNT_B) * CELLS
START_A = COUNT_B * CELLS
HALF = C // 2
GROUP = 25
PACKED = 5 * 128
KEYS = 64
GRAM = (ROWS + 2 * RADIUS) * KEYS
LOG2E = 1.4426950408889634
NT = (((1,), (1,)), ((), ()))


def swap(array, axis, step):
    peers = lax.axis_size(axis)
    pairs = [(i, (i ^ 1) if step == 0 else (i - 1 if i % 2 == 0 else i + 1) % peers) for i in range(peers)]
    return lax.ppermute(array, axis, pairs)


def dot(left, right):
    return jnp.dot(left, right, preferred_element_type=jnp.float32)


MID_A = WIDE_B * ROWS * WIN
MID = (WIDE_B + WIDE_A) * ROWS * WIN
SENT_B = HALO_B * WIN
SENT_A = HALO_A * WIN
SENT = WIDE_B * SENT_B + WIDE_A * SENT_A


def pack_cols(ids, a_ref, b_ref, near_ref, far_ref):
    even = ids[1] % 2 == 0
    for r in range(ROWS):
        a, b = a_ref[r].astype(jnp.float32), b_ref[r].astype(jnp.float32)
        first = jnp.concatenate([b[:HALO_B], a[:HALO_A]], axis=0)
        last = jnp.concatenate([b[-HALO_B:], a[-HALO_A:]], axis=0)
        near_ref[r] = jnp.where(even, last, first).astype(jnp.bfloat16)
        far_ref[r] = jnp.where(even, first, last).astype(jnp.bfloat16)


def pack_rows(ids, a_ref, b_ref, near_ref, far_ref, mid, up_ref, down_ref):
    even = ids[1] % 2 == 0
    for r in range(0, ROWS, 2):
        rows = []
        for k in range(2):
            near = near_ref[r + k].astype(jnp.float32)
            far = far_ref[r + k].astype(jnp.float32)
            before, after = jnp.where(even, far, near), jnp.where(even, near, far)
            a = a_ref[r + k].astype(jnp.float32)
            b = b_ref[r + k].astype(jnp.float32)
            b = jnp.concatenate([before[:HALO_B], b, after[:HALO_B]], axis=0)
            a = jnp.concatenate([before[HALO_B:], a, after[HALO_B:]], axis=0)
            rows.append(jnp.concatenate([b, a], axis=0))
        for j in range(WIDE_B + WIDE_A):
            part = slice(WIN * j, WIN * (j + 1))
            mid[(j * ROWS + r) * WIN : (j * ROWS + r + 2) * WIN] = jnp.concatenate(
                [rows[0][part], rows[1][part]], axis=0
            ).astype(jnp.bfloat16)

    def send(out, last):
        for j in range(WIDE_B):
            start = pl.multiple_of(j * ROWS * WIN + last * (ROWS * WIN - SENT_B), 16)
            out[j * SENT_B : (j + 1) * SENT_B] = mid[pl.ds(start, SENT_B)]
        for j in range(WIDE_A):
            start = pl.multiple_of(MID_A + j * ROWS * WIN + last * (ROWS * WIN - SENT_A), 16)
            at = WIDE_B * SENT_B + j * SENT_A
            out[at : at + SENT_A] = mid[pl.ds(start, SENT_A)]

    odd = ids[0] % 2
    send(up_ref, 1 - odd)
    send(down_ref, odd)


def body(
    ids,
    mid,
    near,
    far,
    gain,
    shift,
    w_k,
    b_k,
    w_qv,
    b_qv,
    bias,
    w_out,
    b_out,
    w_hid,
    w_off,
    b_hid,
    w_flow,
    b_flow,
    mirror,
    unmirror,
    out,
    x_all,
    q_s,
    k_s,
    v_s,
    mix_s,
    fb,
    fa,
    g_s,
    e_s,
):
    def place_rows(above, below):
        for j in range(WIDE_B + WIDE_A):
            if j < WIDE_B:
                at, sent, got = j * HIGH_B * CELLS, SENT_B, j * SENT_B
            else:
                at = START_A + (j - WIDE_B) * HIGH_A * CELLS
                sent, got = SENT_A, WIDE_B * SENT_B + (j - WIDE_B) * SENT_A
            own = ROWS * WIN
            x_all[at : at + sent] = above[got : got + sent]
            x_all[at + sent : at + sent + own] = mid[j * own : (j + 1) * own]
            x_all[at + sent + own : at + 2 * sent + own] = below[got : got + sent]

    even = ids[0] % 2 == 0

    @pl.when(even)
    def _():
        place_rows(far, near)

    @pl.when(jnp.logical_not(even))
    def _():
        place_rows(near, far)

    @pl.loop(0, TOTAL // BLOCK)
    def _(j):
        rows = pl.ds(pl.multiple_of(j * BLOCK, BLOCK), BLOCK)
        x = x_all[rows].astype(jnp.float32)
        centred = x - jnp.mean(x, axis=-1, keepdims=True)
        variance = jnp.mean(centred * centred, axis=-1, keepdims=True)
        normed = centred * lax.rsqrt(variance + 1e-05) * gain[...] + shift[...]
        normed = normed.astype(jnp.bfloat16)
        k_s[rows] = (dot(normed, w_k[...]) + b_k[...]).astype(jnp.bfloat16)
        qv = lax.dot_general(w_qv[...], normed, NT, preferred_element_type=jnp.float32)
        qv = qv + b_qv[...]
        q_s[:, rows] = (qv[:C] * (HEAD**-0.5 * LOG2E)).astype(jnp.bfloat16)
        v_s[:, rows] = qv[C:].astype(jnp.bfloat16)

    place = lax.broadcasted_iota(jnp.int32, (HALF, C), 0) // HEAD
    which = lax.broadcasted_iota(jnp.int32, (HALF, C), 1) // CELLS
    diagonal = (place == which).astype(jnp.float32).astype(jnp.bfloat16)
    low = lax.broadcasted_iota(jnp.int32, (HEAD, 128), 1) < CELLS


    def table_of(window):
        high, wide, inset = HIGH_B, WIDE_B, 1
        if window >= COUNT_B:
            window, high, wide, inset = window - COUNT_B, HIGH_A, WIDE_A, 0
        i, j = window % high, window // high
        index = 0
        for n, at, end in ((0, i, high - 1), (1, j, wide - 1)):
            if at == inset:
                index += (ids[n] == 0).astype(jnp.int32) * (n + 1)
            elif at == end - inset:
                index += (ids[n] == ids[n + 2] - 1).astype(jnp.int32) * (n + 1)
        return bias.at[index]

    def group(first):
        qs, vs, ks = [], [], []
        for u in range(GROUP):
            both = slice((first + u) * 128, (first + u + 1) * 128)
            queries, values = q_s[:, both], v_s[:, both]
            qs += [queries[:, :CELLS], queries[:, CELLS:]]
            vs += [values[:, :CELLS], values[:, CELLS:]]
            keys = k_s[both]
            ks += [keys[:CELLS], keys[CELLS:]]
        scores = []
        for w in range(2 * GROUP):
            for side in range(2):
                part = slice(HALF * side, HALF * (side + 1))
                spread = jnp.concatenate([qs[w][part]] * 4, axis=1) * diagonal
                scores.append(dot(ks[w][:, part], spread))
        weights, scales = [], []
        for w in range(2 * GROUP):
            table = table_of(2 * first + w)
            for side in range(2):
                s = scores[2 * w + side] + table[:, C * side : C * (side + 1)]
                p = jnp.exp2(s - jnp.max(s, axis=0, keepdims=True))
                scales.append(1.0 / jnp.sum(p, axis=0, keepdims=True))
                weights.append(p.astype(jnp.bfloat16))
        results = []
        for w in range(2 * GROUP):
            for side in range(2):
                part = slice(HALF * side, HALF * (side + 1))
                results.append(dot(vs[w][part], weights[2 * w + side]))
        for u in range(GROUP):
            mixed = []
            for head in range(HEADS):
                side, at = head // 4, head % 4
                rows = slice(HEAD * at, HEAD * (at + 1))
                cols = slice(128 * (at // 2), 128 * (at // 2 + 1))
                n = 4 * u + side
                a = results[n][rows, cols] * scales[n][:, cols]
                b = results[n + 2][rows, cols] * scales[n + 2][:, cols]
                if at % 2 == 0:
                    mixed.append(jnp.where(low, a, pltpu.roll(b, CELLS, 1)))
                else:
                    mixed.append(jnp.where(low, pltpu.roll(a, CELLS, 1), b))
            both = slice((first + u) * 128, (first + u + 1) * 128)
            mix_s[both] = jnp.concatenate(mixed, axis=0).T.astype(jnp.bfloat16)

    group(0)

    row_start = ids[0] * ROWS
    col_start = ids[1] * COLS
    total_rows = ids[2] * ROWS
    total_cols = ids[3] * COLS

    def features(x, mixed):
        attended = (dot(mixed, w_out[...]) + b_out[...]).astype(jnp.bfloat16)
        return x.astype(jnp.float32) + attended.astype(jnp.float32)

    col_places = col_start - HALO_B + lax.broadcasted_iota(jnp.int32, (KEYS, 1), 0)
    col_inside = (col_places >= 0) & (col_places < total_cols)
    blank = jnp.zeros((KEYS - WIDE_B * WIN, C), jnp.float32)

    def gather(ref, start, high, wide, i):
        return jnp.concatenate(
            [ref[pl.ds(start + (j * high + i) * CELLS, CELLS)] for j in range(wide)], axis=0
        )

    strips = [(0, HIGH_B, WIDE_B, i) for i in range(HIGH_B)]
    strips += [(START_A, HIGH_A, WIDE_A, i) for i in range(HIGH_A)]
    sums = [dot(gather(mix_s, *strip), w_out[...]) for strip in strips]
    for strip, total in zip(strips, sums):
        i = strip[-1]
        attended = (total + b_out[...]).astype(jnp.bfloat16)
        f = gather(x_all, *strip).astype(jnp.float32) + attended.astype(jnp.float32)
        if strip[0] == START_A:
            f = dot(mirror[...], f.astype(jnp.bfloat16)).astype(jnp.bfloat16)
            fa[i * WIN * COLS : (i + 1) * WIN * COLS] = f
            continue
        for r in range(WIN):
            row = jnp.concatenate(
                [f[CELLS * j + WIN * r : CELLS * j + WIN * (r + 1)] for j in range(WIDE_B)]
                + [blank],
                axis=0,
            )
            at = i * WIN + r
            place = row_start - HALO_B + at
            inside = col_inside & (place >= 0) & (place < total_rows)
            fb[at * KEYS : (at + 1) * KEYS] = jnp.where(inside, row, 0.0).astype(jnp.bfloat16)

    lane = lax.broadcasted_iota(jnp.int32, (COLS, 128), 1)
    near = lane % 32 < SPAN
    early = lane % KEYS < 32
    first = near & (lane < 32)
    second = near & (lane >= 32)

    for n in range(4):
        top, end = max(0, 8 * n - 16), min(ROWS, 8 * n + 8)
        queries = fa[(HALO_A + top) * COLS : (HALO_A + end) * COLS]
        start = (HALO_B - RADIUS + 8 * n) * KEYS
        keys = fb[start : start + 8 * KEYS]
        g_s[top * COLS : end * COLS, 8 * KEYS * n : 8 * KEYS * (n + 1)] = lax.dot_general(
            queries, keys, NT, preferred_element_type=jnp.float32
        )

    def align(r, n):
        at = 128 * (n + r // 2)
        tile = g_s[COLS * r : COLS * (r + 1), at : at + 128]
        turn = 128 - HALO_A - COLS + 1 - 32 * (n % 2)
        return pltpu.roll(tile, turn, 1, stride=1, stride_axis=0)

    for r in range(ROWS):
        tiles = []
        for n in range(5):
            tile = align(r, 2 * n)
            if n < 4:
                tile = jnp.where(early, tile, align(r, 2 * n + 1))
            keep = near
            if r % 2 == 0 and n == 4:
                keep = first
            if r % 2 == 1 and n == 0:
                keep = second
            if n == 4 and r % 2 == 1:
                keep = near & early
            tiles.append(jnp.where(keep, tile * (C**-0.5 * LOG2E), -1e30))
        most = tiles[0]
        for tile in tiles[1:]:
            most = jnp.maximum(most, tile)
        most = jnp.max(most, axis=-1, keepdims=True)
        rows = slice((r // 2) * COLS, (r // 2 + 1) * COLS)
        for n in range(5):
            e_s[r % 2, rows, 128 * n : 128 * (n + 1)] = jnp.exp2(tiles[n] - most).astype(
                jnp.bfloat16
            )

    sums = [dot(e_s[par], w_off[par]) for par in range(2)]
    hidden = [dot(e_s[par], w_hid[par]) for par in range(2)]
    flows = []
    for par in range(2):
        scale = 1.0 / sums[par][:, 2:3]
        act = jax.nn.gelu(hidden[par] * (scale * OFFS) + b_hid[...]).astype(jnp.bfloat16)
        flow = sums[par] * scale + dot(act, w_flow[...]) + b_flow[...]
        flows.append(flow.T[:WIN])
    flow = jnp.concatenate(flows, axis=0)
    high = flow.astype(jnp.bfloat16)
    rest = flow - high.astype(jnp.float32)
    mid = rest.astype(jnp.bfloat16)
    tail = (rest - mid.astype(jnp.float32)).astype(jnp.bfloat16)
    flow = dot(high, unmirror[...]) + dot(mid, unmirror[...]) + dot(tail, unmirror[...])
    for r in range(ROWS):
        at = WIN * (r % 2)
        out[:, r, :] = flow[at : at + 2, COLS * (r // 2) : COLS * (r // 2 + 1)]


def places():
    lanes = np.zeros((2, SPAN, SPAN), np.int64)
    for par in range(2):
        for dr in range(SPAN):
            row = dr + par
            tile, half = row // 2, row % 2
            slot = 2 * half if tile % 2 == 0 else 3 - 2 * half
            lanes[par, dr] = 128 * (tile // 2) + 32 * slot + np.arange(SPAN)
    return lanes.reshape(2, OFFS)


def skewed(w_hid):
    pick = np.zeros((2, PACKED, OFFS), np.float32)
    for par, lanes in enumerate(places()):
        pick[par, lanes, np.arange(OFFS)] = 1.0
    pick = jnp.asarray(pick.reshape(2 * PACKED, OFFS), jnp.bfloat16)
    return dot(pick, w_hid).astype(jnp.bfloat16).reshape(2, PACKED, C)


def offsets():
    table = np.zeros((2, PACKED, 128), np.float32)
    offs = np.arange(OFFS)
    for par, lanes in enumerate(places()):
        table[par, lanes, 0] = offs // SPAN - RADIUS
        table[par, lanes, 1] = offs % SPAN - RADIUS
        table[par, lanes, 2] = 1.0
    return jnp.asarray(table, jnp.bfloat16)


def mirrors():
    turn = np.zeros((WIN, COLS, WIDE_A, WIN, WIN), np.float32)
    for r in range(WIN):
        for c in range(COLS):
            place = HALO_A + COLS - 1 - c
            turn[r, c, place // WIN, r, place % WIN] = 1.0
    turn = jnp.asarray(turn.reshape(WIN * COLS, WIDE_A * CELLS), jnp.bfloat16)
    back = np.kron(np.eye(ROWS // 2, dtype=np.float32), np.eye(COLS, dtype=np.float32)[::-1])
    return turn, jnp.asarray(back, jnp.bfloat16)


def position_bias(rel_table):
    places = np.arange(CELLS)
    rows, cols = places // WIN, places % WIN
    index = (rows[:, None] - rows[None, :] + WIN - 1) * (2 * WIN - 1) + (
        cols[:, None] - cols[None, :] + WIN - 1
    )
    pick = np.zeros(((2 * WIN - 1) ** 2, CELLS * CELLS), np.float32)
    pick[index.reshape(-1), np.arange(CELLS * CELLS)] = 1.0
    pick = jnp.asarray(pick, jnp.bfloat16)
    high = rel_table.astype(jnp.bfloat16)
    rest = rel_table - high.astype(jnp.float32)
    mid = rest.astype(jnp.bfloat16)
    low = (rest - mid.astype(jnp.float32)).astype(jnp.bfloat16)
    table = jnp.sum(
        dot(jnp.concatenate([high, mid, low], axis=0), pick).reshape(3, HEADS, CELLS, CELLS),
        axis=0,
    )
    split_r = (rows[:, None] < SHIFT) != (rows[None, :] < SHIFT)
    split_c = (cols[:, None] < SHIFT) != (cols[None, :] < SHIFT)
    masks = np.stack([split_r & False, split_r, split_c, split_r | split_c])
    masks = jnp.asarray(np.where(masks, -100.0, 0.0), jnp.float32)
    full = (table.transpose(2, 0, 1)[None] + masks[:, :, None, :]) * LOG2E
    return full.reshape(4, CELLS, HEADS * CELLS)


def shards(
    section_a,
    section_b,
    ln_gain,
    ln_shift,
    w_qkv,
    b_qkv,
    rel_table,
    w_out,
    b_out,
    w_hid,
    b_hid,
    w_flow,
    b_flow,
):
    ids = jnp.stack(
        [
            lax.axis_index("row"),
            lax.axis_index("col"),
            jnp.int32(lax.axis_size("row")),
            jnp.int32(lax.axis_size("col")),
        ]
    )
    scalars = pl.BlockSpec(memory_space=pltpu.SMEM)
    whole = pl.BlockSpec(memory_space=pltpu.VMEM)
    strip = jax.ShapeDtypeStruct((ROWS, HALO_A + HALO_B, C), jnp.bfloat16)
    near, far = pl.pallas_call(
        pack_cols,
        out_shape=(strip, strip),
        in_specs=[scalars, whole, whole],
        out_specs=(whole, whole),
    )(ids, section_a, section_b)
    near, far = swap(near, "col", 0), swap(far, "col", 1)
    sent = jax.ShapeDtypeStruct((SENT, C), jnp.bfloat16)
    mid, near, far = pl.pallas_call(
        pack_rows,
        out_shape=(jax.ShapeDtypeStruct((MID, C), jnp.bfloat16), sent, sent),
        in_specs=[scalars] + [whole] * 4,
        out_specs=(whole,) * 3,
    )(ids, section_a, section_b, near, far)
    near, far = swap(near, "row", 0), swap(far, "row", 1)

    w_qv = jnp.concatenate([w_qkv[:, :C], w_qkv[:, 2 * C :]], axis=1).T
    b_qv = jnp.concatenate([b_qkv[:C], b_qkv[2 * C :]])[:, None]

    flow_pad = jnp.pad(w_flow, ((0, 0), (0, 126)))
    b_flow_pad = jnp.pad(b_flow, (0, 126))
    call = pl.pallas_call(
        body,
        out_shape=jax.ShapeDtypeStruct((2, ROWS, COLS), jnp.float32),
        in_specs=[scalars] + [whole] * 19,
        out_specs=whole,
        scratch_shapes=[
            pltpu.VMEM((TOTAL, C), jnp.bfloat16),
            pltpu.VMEM((C, TOTAL), jnp.bfloat16),
            pltpu.VMEM((TOTAL, C), jnp.bfloat16),
            pltpu.VMEM((C, TOTAL), jnp.bfloat16),
            pltpu.VMEM((TOTAL, C), jnp.bfloat16),
            pltpu.VMEM((HIGH_B * WIN * KEYS, C), jnp.bfloat16),
            pltpu.VMEM((HIGH_A * WIN * COLS, C), jnp.bfloat16),
            pltpu.VMEM((ROWS * COLS, GRAM), jnp.float32),
            pltpu.VMEM((2, ROWS // 2 * COLS, PACKED), jnp.bfloat16),
        ],
        compiler_params=pltpu.CompilerParams(vmem_limit_bytes=40 * 1024 * 1024),
    )
    return call(
        ids,
        mid,
        near,
        far,
        ln_gain[None],
        ln_shift[None],
        w_qkv[:, C : 2 * C],
        b_qkv[None, C : 2 * C],
        w_qv,
        b_qv,
        position_bias(rel_table),
        w_out,
        b_out[None],
        skewed(w_hid),
        offsets(),
        b_hid[None],
        flow_pad,
        b_flow_pad[None],
        *mirrors(),
    )


def solution(mesh):
    placed = (P("row", "col", None),) * 2 + (P(),) * 11
    return jax.shard_map(
        shards, mesh=mesh, in_specs=placed, out_specs=P(None, "row", "col"), check_vma=False
    )
```

```python
import jax
import jax.numpy as jnp
from jax import lax
from jax.experimental import pallas as pl
from jax.experimental.pallas import tpu as pltpu
from jax.sharding import PartitionSpec as P

C = 256
HEADS = 8
HEAD = 32
WIN = 8
SHIFT = 4
RADIUS = 8
SPAN = 2 * RADIUS + 1
OFFS = SPAN * SPAN
ROWS = 16
COLS = 32
HALO_A = 4
HALO_B = 12
HIGH_A, WIDE_A = 3, 5
HIGH_B, WIDE_B = 5, 7
CELLS = WIN * WIN
STRIPS_A, STRIPS_B = (0, 2), (0, 1, 3, 4)
LEFT_A, LEFT_B = len(STRIPS_A), len(STRIPS_B)
START_A = LEFT_B * WIDE_B * CELLS
TOTAL = START_A + LEFT_A * WIDE_A * CELLS
HALF = C // 2
PACKED = 5 * 128
KEYS = 64
GRAM = (ROWS + 2 * RADIUS) * KEYS
LOG2E = 1.4426950408889634
NT = (((1,), (1,)), ((), ()))


def swap(array, axis, step):
    peers = lax.axis_size(axis)
    pairs = [(i, (i ^ 1) if step == 0 else (i - 1 if i % 2 == 0 else i + 1) % peers) for i in range(peers)]
    return lax.ppermute(array, axis, pairs)


def dot(left, right):
    return jnp.dot(left, right, preferred_element_type=jnp.float32)


MID_A = WIDE_B * ROWS * WIN
MID = (WIDE_B + WIDE_A) * ROWS * WIN
SENT_B = HALO_B * WIN
SENT_A = HALO_A * WIN
SENT = WIDE_B * SENT_B + WIDE_A * SENT_A


def pack_cols(ids, a_ref, b_ref, far_ref, near_ref):
    even = ids[1] % 2 == 0
    for r in range(ROWS):
        a, b = a_ref[r].astype(jnp.float32), b_ref[r].astype(jnp.float32)
        first = jnp.concatenate([b[:HALO_B], a[:HALO_A]], axis=0)
        last = jnp.concatenate([b[-HALO_B:], a[-HALO_A:]], axis=0)
        near_ref[r] = jnp.where(even, last, first).astype(jnp.bfloat16)
        far_ref[r] = jnp.where(even, first, last).astype(jnp.bfloat16)


def pack_rows(ids, a_ref, b_ref, far_ref, near_ref, mid, down_ref, up_ref):
    even = ids[1] % 2 == 0
    for r in range(0, ROWS, 2):
        rows = []
        for k in range(2):
            near = near_ref[r + k].astype(jnp.float32)
            far = far_ref[r + k].astype(jnp.float32)
            before, after = jnp.where(even, far, near), jnp.where(even, near, far)
            a = a_ref[r + k].astype(jnp.float32)
            b = b_ref[r + k].astype(jnp.float32)
            b = jnp.concatenate([before[:HALO_B], b, after[:HALO_B]], axis=0)
            a = jnp.concatenate([before[HALO_B:], a, after[HALO_B:]], axis=0)
            rows.append(jnp.concatenate([b, a], axis=0))
        for j in range(WIDE_B + WIDE_A):
            part = slice(WIN * j, WIN * (j + 1))
            mid[(j * ROWS + r) * WIN : (j * ROWS + r + 2) * WIN] = jnp.concatenate(
                [rows[0][part], rows[1][part]], axis=0
            ).astype(jnp.bfloat16)

    def send(out, last):
        for j in range(WIDE_B):
            start = pl.multiple_of(j * ROWS * WIN + last * (ROWS * WIN - SENT_B), 16)
            out[j * SENT_B : (j + 1) * SENT_B] = mid[pl.ds(start, SENT_B)]
        for j in range(WIDE_A):
            start = pl.multiple_of(MID_A + j * ROWS * WIN + last * (ROWS * WIN - SENT_A), 16)
            at = WIDE_B * SENT_B + j * SENT_A
            out[at : at + SENT_A] = mid[pl.ds(start, SENT_A)]

    odd = ids[0] % 2
    send(up_ref, 1 - odd)
    send(down_ref, odd)


def normalise(x, gain, shift):
    x = x.astype(jnp.float32)
    centred = x - jnp.mean(x, axis=-1, keepdims=True)
    variance = jnp.mean(centred * centred, axis=-1, keepdims=True)
    normed = centred * lax.rsqrt(variance + 1e-05) * gain[...] + shift[...]
    return normed.astype(jnp.bfloat16)


def project(normed, rows, w_qkv, b_qkv, w_qv, b_qv, q_s, k_s, v_s):
    k_s[rows] = (dot(normed, w_qkv[:, C : 2 * C]) + b_qkv[:, C : 2 * C]).astype(jnp.bfloat16)
    qv = lax.dot_general(w_qv[...], normed, NT, preferred_element_type=jnp.float32)
    qv = qv + b_qv[:, :1]
    q_s[:, rows] = (qv[:C] * (HEAD**-0.5 * LOG2E)).astype(jnp.bfloat16)
    v_s[:, rows] = qv[C:].astype(jnp.bfloat16)


def table_of(ids, bias, i, j, high, wide, inset):
    index = 0
    for n, at, end in ((0, i, high - 1), (1, j, wide - 1)):
        if at == inset:
            index += (ids[n] == 0).astype(jnp.int32) * (n + 1)
        elif at == end - inset:
            index += (ids[n] == ids[n + 2] - 1).astype(jnp.int32) * (n + 1)
    return bias.at[index]


def attend(tables, q_s, k_s, v_s, mix_s):
    place = lax.broadcasted_iota(jnp.int32, (HALF, C), 0) // HEAD
    which = lax.broadcasted_iota(jnp.int32, (HALF, C), 1) // CELLS
    diagonal = (place == which).astype(jnp.float32).astype(jnp.bfloat16)
    low = lax.broadcasted_iota(jnp.int32, (HEAD, 128), 1) < CELLS
    pairs = [slice(128 * u, 128 * (u + 1)) for u in range(len(tables) // 2)]
    sides = [slice(HALF * side, HALF * (side + 1)) for side in range(2)]
    qs, ks, vs = [], [], []
    for both in pairs:
        queries, values, keys = q_s[:, both], v_s[:, both], k_s[both]
        qs += [queries[:, :CELLS], queries[:, CELLS:]]
        vs += [values[:, :CELLS], values[:, CELLS:]]
        ks += [keys[:CELLS], keys[CELLS:]]
    scores = []
    for q, k in zip(qs, ks):
        for part in sides:
            spread = jnp.concatenate([q[part]] * 4, axis=1) * diagonal
            scores.append(dot(k[:, part], spread))
    weights, scales = [], []
    for w, table in enumerate(tables):
        for side in range(2):
            s = scores[2 * w + side] + table[:, C * side : C * (side + 1)]
            p = jnp.exp2(s - jnp.max(s, axis=0, keepdims=True))
            scales.append(1.0 / jnp.sum(p, axis=0, keepdims=True))
            weights.append(p.astype(jnp.bfloat16))
    results = []
    for w, v in enumerate(vs):
        for side, part in enumerate(sides):
            results.append(dot(v[part], weights[2 * w + side]))
    for u, both in enumerate(pairs):
        mixed = []
        for head in range(HEADS):
            side, at = head // 4, head % 4
            rows = slice(HEAD * at, HEAD * (at + 1))
            cols = slice(128 * (at // 2), 128 * (at // 2 + 1))
            n = 4 * u + side
            a = results[n][rows, cols] * scales[n][:, cols]
            b = results[n + 2][rows, cols] * scales[n + 2][:, cols]
            if at % 2 == 0:
                mixed.append(jnp.where(low, a, pltpu.roll(b, CELLS, 1)))
            else:
                mixed.append(jnp.where(low, pltpu.roll(a, CELLS, 1), b))
        mix_s[both] = jnp.concatenate(mixed, axis=0).T.astype(jnp.bfloat16)


def column(ref, start, high, wide, t):
    return jnp.concatenate(
        [ref[start + (j * high + t) * CELLS : start + (j * high + t + 1) * CELLS] for j in range(wide)],
        axis=0,
    )


def finish(ids, x, total, b_out, mirror, strip, out, at):
    f = x.astype(jnp.float32) + (total + b_out[...]).astype(jnp.bfloat16).astype(jnp.float32)
    if strip is None:
        out[at : at + WIN * COLS] = dot(mirror[...], f.astype(jnp.bfloat16)).astype(jnp.bfloat16)
        return
    row_start, col_start = ids[0] * ROWS - HALO_B, ids[1] * COLS - HALO_B
    col_places = col_start + lax.broadcasted_iota(jnp.int32, (KEYS, 1), 0)
    col_inside = (col_places >= 0) & (col_places < ids[3] * COLS)
    blank = jnp.zeros((KEYS - WIDE_B * WIN, C), jnp.float32)
    for r in range(WIN):
        row = jnp.concatenate(
            [f[CELLS * j + WIN * r : CELLS * j + WIN * (r + 1)] for j in range(WIDE_B)] + [blank],
            axis=0,
        )
        place = row_start + strip * WIN + r
        inside = col_inside & (place >= 0) & (place < ids[2] * ROWS)
        out[at + r * KEYS : at + (r + 1) * KEYS] = jnp.where(inside, row, 0.0).astype(jnp.bfloat16)


def centre(
    ids, mid, gain, shift, w_qkv, b_qkv, w_qv, b_qv, bias, w_out, b_out, mirror,
    outer, fb, fa, q_s, k_s, v_s, mix_s,
):
    x_s = []
    for j in range(0, WIDE_B + WIDE_A, 4):
        inner = []
        for n in range(j, j + 4):
            at = n * ROWS * WIN
            normed = normalise(mid[at : at + ROWS * WIN], gain, shift)
            outer[n * CELLS : n * CELLS + SENT_A] = normed[:SENT_A]
            outer[n * CELLS + SENT_A : (n + 1) * CELLS] = normed[-SENT_A:]
            inner.append(normed[SENT_A:-SENT_A])
            x_s.append(mid[at + SENT_A : at + SENT_A + CELLS])
        rows = slice(j * CELLS, (j + 4) * CELLS)
        project(jnp.concatenate(inner, axis=0), rows, w_qkv, b_qkv, w_qv, b_qv, q_s, k_s, v_s)
    tables = [table_of(ids, bias, 2, j, HIGH_B, WIDE_B, 1) for j in range(WIDE_B)]
    tables += [table_of(ids, bias, 1, j, HIGH_A, WIDE_A, 0) for j in range(WIDE_A)]
    attend(tables, q_s, k_s, v_s, mix_s)
    cut = WIDE_B * CELLS
    sum_b, sum_a = dot(mix_s[:cut], w_out[...]), dot(mix_s[cut:], w_out[...])
    finish(ids, jnp.concatenate(x_s[:WIDE_B], axis=0), sum_b, b_out, mirror, 2, fb, 0)
    finish(ids, jnp.concatenate(x_s[WIDE_B:], axis=0), sum_a, b_out, mirror, None, fa, 0)


def body(
    ids,
    mid,
    far,
    near,
    outer,
    centre_b,
    centre_a,
    gain,
    shift,
    w_qkv,
    b_qkv,
    w_qv,
    b_qv,
    bias,
    w_out,
    b_out,
    w_hid,
    w_off,
    b_hid,
    w_flow,
    b_flow,
    mirror,
    unmirror,
    out,
    x_s,
    q_s,
    k_s,
    v_s,
    mix_s,
    fb,
    fa,
    g_s,
    e_s,
):
    def spans():
        for j in range(WIDE_B + WIDE_A):
            if j < WIDE_B:
                yield j, j * LEFT_B * CELLS, SENT_B, j * SENT_B
            else:
                n = j - WIDE_B
                yield j, START_A + n * LEFT_A * CELLS, SENT_A, WIDE_B * SENT_B + n * SENT_A

    def place_rows(above, below):
        for j, at, sent, got in spans():
            own = j * ROWS * WIN
            x_s[at : at + sent] = above[got : got + sent]
            x_s[at + sent : at + sent + SENT_A] = mid[own : own + SENT_A]
            x_s[at + sent + SENT_A : at + sent + CELLS] = mid[
                own + ROWS * WIN - SENT_A : own + ROWS * WIN
            ]
            x_s[at + sent + CELLS : at + 2 * sent + CELLS] = below[got : got + sent]

    even = ids[0] % 2 == 0

    @pl.when(even)
    def _():
        place_rows(far, near)

    @pl.when(jnp.logical_not(even))
    def _():
        place_rows(near, far)

    normed, start = [], 0
    for j, at, sent, _ in spans():
        top = normalise(x_s[at : at + sent], gain, shift)
        low = normalise(x_s[at + sent + CELLS : at + 2 * sent + CELLS], gain, shift)
        normed += [top, outer[j * CELLS : (j + 1) * CELLS], low]
        end = at + 2 * sent + CELLS
        if j % 2 == 1 or j == WIDE_B + WIDE_A - 1:
            rows = slice(start, end)
            project(jnp.concatenate(normed, axis=0), rows, w_qkv, b_qkv, w_qv, b_qv, q_s, k_s, v_s)
            normed, start = [], end

    tables = [
        table_of(ids, bias, i, j, HIGH_B, WIDE_B, 1) for j in range(WIDE_B) for i in STRIPS_B
    ] + [table_of(ids, bias, i, j, HIGH_A, WIDE_A, 0) for j in range(WIDE_A) for i in STRIPS_A]
    attend(tables, q_s, k_s, v_s, mix_s)

    strips = [(0, LEFT_B, WIDE_B, t) for t in range(LEFT_B)]
    strips += [(START_A, LEFT_A, WIDE_A, t) for t in range(LEFT_A)]
    sums = [dot(column(mix_s, *strip), w_out[...]) for strip in strips]
    for strip, total in zip(strips, sums):
        x, t = column(x_s, *strip), strip[-1]
        if strip[0] == START_A:
            finish(ids, x, total, b_out, mirror, None, fa, STRIPS_A[t] * WIN * COLS)
        else:
            i = STRIPS_B[t]
            finish(ids, x, total, b_out, mirror, i, fb, i * WIN * KEYS)
    fb[2 * WIN * KEYS : 3 * WIN * KEYS] = centre_b[...]
    fa[WIN * COLS : 2 * WIN * COLS] = centre_a[...]

    lane = lax.broadcasted_iota(jnp.int32, (COLS, 128), 1)
    valid = lane % 32 < SPAN
    early = lane % KEYS < 32
    first = valid & (lane < 32)
    second = valid & (lane >= 32)

    for n in range(4):
        top, end = max(0, 8 * n - 16), min(ROWS, 8 * n + 8)
        queries = fa[(HALO_A + top) * COLS : (HALO_A + end) * COLS]
        start = (HALO_B - RADIUS + 8 * n) * KEYS
        keys = fb[start : start + 8 * KEYS]
        g_s[top * COLS : end * COLS, 8 * KEYS * n : 8 * KEYS * (n + 1)] = lax.dot_general(
            queries, keys, NT, preferred_element_type=jnp.float32
        )

    def align(r, n):
        at = 128 * (n + r // 2)
        tile = g_s[COLS * r : COLS * (r + 1), at : at + 128]
        turn = 128 - HALO_A - COLS + 1 - 32 * (n % 2)
        return pltpu.roll(tile, turn, 1, stride=1, stride_axis=0)

    for r in range(ROWS):
        tiles = []
        for n in range(5):
            tile = align(r, 2 * n)
            if n < 4:
                tile = jnp.where(early, tile, align(r, 2 * n + 1))
            keep = valid
            if r % 2 == 0 and n == 4:
                keep = first
            if r % 2 == 1 and n == 0:
                keep = second
            if n == 4 and r % 2 == 1:
                keep = valid & early
            tiles.append(jnp.where(keep, tile * (C**-0.5 * LOG2E), -1e30))
        most = tiles[0]
        for tile in tiles[1:]:
            most = jnp.maximum(most, tile)
        most = jnp.max(most, axis=-1, keepdims=True)
        rows = slice((r // 2) * COLS, (r // 2 + 1) * COLS)
        for n in range(5):
            e_s[r % 2, rows, 128 * n : 128 * (n + 1)] = jnp.exp2(tiles[n] - most).astype(
                jnp.bfloat16
            )

    sums = [dot(e_s[par], w_off[par * PACKED : (par + 1) * PACKED]) for par in range(2)]
    hidden = [dot(e_s[par], w_hid[par * PACKED : (par + 1) * PACKED]) for par in range(2)]
    flows = []
    for par in range(2):
        scale = 1.0 / sums[par][:, 2:3]
        act = jax.nn.gelu(hidden[par] * (scale * OFFS) + b_hid[...]).astype(jnp.bfloat16)
        flow = sums[par] * scale + dot(act, w_flow[...]) + b_flow[...]
        flows.append(flow.T[:WIN])
    flow = jnp.concatenate(flows, axis=0)
    high = flow.astype(jnp.bfloat16)
    rest = flow - high.astype(jnp.float32)
    mid = rest.astype(jnp.bfloat16)
    tail = (rest - mid.astype(jnp.float32)).astype(jnp.bfloat16)
    flow = dot(high, unmirror[...]) + dot(mid, unmirror[...]) + dot(tail, unmirror[...])
    for r in range(ROWS):
        at = WIN * (r % 2)
        out[:, r, :] = flow[at : at + 2, COLS * (r // 2) : COLS * (r // 2 + 1)]


def prepare(
    w_qkv, b_qkv, w_hid, w_flow, b_flow, rel,
    w_qv, b_qv, packed, flow_w, flow_b, bias, w_off, turn, back,
):
    def iota(shape, dim):
        return lax.broadcasted_iota(jnp.int32, shape, dim)

    def onehot(hit):
        return hit.astype(jnp.float32).astype(jnp.bfloat16)

    lane = iota((2 * PACKED, 1), 0)
    par = (lane >= PACKED).astype(jnp.int32)
    lane = lane - par * PACKED
    slot, dc = lane % 128 // 32, lane % 32
    dr = lane // 128 * 4 + jnp.where(slot == 1, 3, jnp.where(slot == 3, 2, slot // 2)) - par
    inside = (dr >= 0) & (dr < SPAN) & (dc < SPAN)
    place = jnp.where(inside, dr * SPAN + dc, -1)
    pick = onehot(iota((2 * PACKED, OFFS), 1) == place)
    which = iota((2 * PACKED, 128), 1)
    offs = jnp.where(which == 0, dr - RADIUS, jnp.where(which == 1, dc - RADIUS, 1))
    offs = jnp.where(inside & (which < 3), offs, 0)
    w_off[...] = offs.astype(jnp.float32).astype(jnp.bfloat16)
    at = iota(turn.shape, 0)
    col = HALO_A + COLS - 1 - at % COLS
    source = col // WIN * CELLS + at // COLS * WIN + col % WIN
    turn[...] = onehot(iota(turn.shape, 1) == source)
    at = iota(back.shape, 0)
    back[...] = onehot(iota(back.shape, 1) == at // COLS * COLS + COLS - 1 - at % COLS)
    side = 2 * WIN - 1
    at = iota((side * side, C), 0)
    spread = onehot(iota(at.shape, 1) == 16 * (at // side + 1) + at % side)
    at = iota((C, 128), 0)
    cell = at % 128 // 16 * WIN + at % 16
    squeeze = onehot((at % 16 < WIN) & (iota(at.shape, 1) == at // 128 * CELLS + cell))

    w_qv[:C] = w_qkv[:, :C].T
    w_qv[C:] = w_qkv[:, 2 * C :].T
    b = b_qkv[...]
    b = jnp.concatenate([b[:, :C], b[:, 2 * C :]], axis=1)
    b_qv[...] = jnp.broadcast_to(b, (128, 2 * C)).T
    packed[...] = dot(pick, w_hid[...]).astype(jnp.bfloat16)
    flow_w[...] = jnp.concatenate(
        [w_flow[...].astype(jnp.float32), jnp.zeros((C, 126), jnp.float32)], axis=1
    ).astype(jnp.bfloat16)
    flow_b[...] = jnp.concatenate([b_flow[...], jnp.zeros((1, 126), jnp.float32)], axis=1)

    def exactly(x, onehot):
        high = x.astype(jnp.bfloat16)
        rest = x - high.astype(jnp.float32)
        mid = rest.astype(jnp.bfloat16)
        low = (rest - mid.astype(jnp.float32)).astype(jnp.bfloat16)
        return dot(high, onehot) + dot(mid, onehot) + dot(low, onehot)

    table = exactly(rel[...], spread) * LOG2E
    parts = []
    for head in range(HEADS):
        line = jnp.broadcast_to(table[head : head + 1], (WIN, C))
        rows = []
        for r in range(WIN):
            start = 16 * (WIN - r) - 1
            rows.append(pltpu.roll(line[:, start : start + 128], 120, 1, stride=1, stride_axis=0))
        parts.append(jnp.concatenate(rows, axis=0))
    pairs = [
        exactly(jnp.concatenate(parts[2 * p : 2 * p + 2], axis=1), squeeze)
        for p in range(HEADS // 2)
    ]
    base = jnp.concatenate(pairs, axis=1)
    key = lax.broadcasted_iota(jnp.int32, base.shape, 0)
    query = lax.broadcasted_iota(jnp.int32, base.shape, 1) % CELLS
    rows = (key // WIN < SHIFT) != (query // WIN < SHIFT)
    cols = (key % WIN < SHIFT) != (query % WIN < SHIFT)
    far = base - 100.0 * LOG2E
    bias[0] = base
    bias[1] = jnp.where(rows, far, base)
    bias[2] = jnp.where(cols, far, base)
    bias[3] = jnp.where(rows | cols, far, base)


def shards(
    section_a,
    section_b,
    ln_gain,
    ln_shift,
    w_qkv,
    b_qkv,
    rel_table,
    w_out,
    b_out,
    w_hid,
    b_hid,
    w_flow,
    b_flow,
):
    ids = jnp.stack(
        [
            lax.axis_index("row"),
            lax.axis_index("col"),
            jnp.int32(lax.axis_size("row")),
            jnp.int32(lax.axis_size("col")),
        ]
    )
    scalars = pl.BlockSpec(memory_space=pltpu.SMEM)
    whole = pl.BlockSpec(memory_space=pltpu.VMEM)
    params = pltpu.CompilerParams(vmem_limit_bytes=40 * 1024 * 1024)
    def made(*shape):
        return jax.ShapeDtypeStruct(shape, jnp.bfloat16)

    def made_f32(*shape):
        return jax.ShapeDtypeStruct(shape, jnp.float32)

    made_ready = pl.pallas_call(
        prepare,
        out_shape=(
            made(2 * C, C),
            made_f32(2 * C, 128),
            made(2 * PACKED, C),
            made(C, 128),
            made_f32(1, 128),
            made_f32(4, CELLS, HEADS * CELLS),
            made(2 * PACKED, 128),
            made(WIN * COLS, WIDE_A * CELLS),
            made(C, C),
        ),
        in_specs=[whole] * 6,
        out_specs=(whole,) * 9,
        compiler_params=params,
        cost_estimate=pl.CostEstimate(flops=10**9, bytes_accessed=4 * 10**6, transcendentals=0),
    )(w_qkv, b_qkv[None], w_hid, w_flow, b_flow[None], rel_table)
    strip = jax.ShapeDtypeStruct((ROWS, HALO_A + HALO_B, C), jnp.bfloat16)
    far, near = pl.pallas_call(
        pack_cols,
        out_shape=(strip, strip),
        in_specs=[scalars, whole, whole],
        out_specs=(whole, whole),
        compiler_params=params,
    )(ids, section_a, section_b)
    far = swap(far, "col", 1)
    near = swap(near, "col", 0)
    far, near, made_ready = lax.optimization_barrier((far, near, made_ready))
    w_qv, b_qv, packed, flow_pad, b_flow_pad, bias, w_off, turn, back = made_ready
    sent = jax.ShapeDtypeStruct((SENT, C), jnp.bfloat16)
    mid, far, near = pl.pallas_call(
        pack_rows,
        out_shape=(jax.ShapeDtypeStruct((MID, C), jnp.bfloat16), sent, sent),
        in_specs=[scalars] + [whole] * 4,
        out_specs=(whole,) * 3,
        compiler_params=params,
    )(ids, section_a, section_b, far, near)
    far = swap(far, "row", 1)
    near = swap(near, "row", 0)

    side = (WIDE_B + WIDE_A) * CELLS
    tables = (ln_gain[None], ln_shift[None], w_qkv, b_qkv[None], w_qv, b_qv, bias, w_out, b_out[None])
    outer, centre_b, centre_a = pl.pallas_call(
        centre,
        out_shape=(made(side, C), made(WIN * KEYS, C), made(WIN * COLS, C)),
        in_specs=[scalars] + [whole] * 11,
        out_specs=(whole,) * 3,
        scratch_shapes=[
            pltpu.VMEM((C, side), jnp.bfloat16),
            pltpu.VMEM((side, C), jnp.bfloat16),
            pltpu.VMEM((C, side), jnp.bfloat16),
            pltpu.VMEM((side, C), jnp.bfloat16),
        ],
        compiler_params=params,
        cost_estimate=pl.CostEstimate(flops=2 * 10**9, bytes_accessed=4 * 10**6, transcendentals=0),
    )(ids, mid, *tables, turn)

    call = pl.pallas_call(
        body,
        out_shape=jax.ShapeDtypeStruct((2, ROWS, COLS), jnp.float32),
        in_specs=[scalars] + [whole] * 22,
        out_specs=whole,
        scratch_shapes=[
            pltpu.VMEM((TOTAL, C), jnp.bfloat16),
            pltpu.VMEM((C, TOTAL), jnp.bfloat16),
            pltpu.VMEM((TOTAL, C), jnp.bfloat16),
            pltpu.VMEM((C, TOTAL), jnp.bfloat16),
            pltpu.VMEM((TOTAL, C), jnp.bfloat16),
            pltpu.VMEM((HIGH_B * WIN * KEYS, C), jnp.bfloat16),
            pltpu.VMEM((HIGH_A * WIN * COLS, C), jnp.bfloat16),
            pltpu.VMEM((ROWS * COLS, GRAM), jnp.float32),
            pltpu.VMEM((2, ROWS // 2 * COLS, PACKED), jnp.bfloat16),
        ],
        compiler_params=params,
    )
    return call(
        ids,
        mid,
        far,
        near,
        outer,
        centre_b,
        centre_a,
        *tables,
        packed,
        w_off,
        b_hid[None],
        flow_pad,
        b_flow_pad,
        turn,
        back,
    )


def solution(mesh):
    placed = (P("row", "col", None),) * 2 + (P(),) * 11
    return jax.shard_map(
        shards, mesh=mesh, in_specs=placed, out_specs=P(None, "row", "col"), check_vma=False
    )
```

```python
import jax
import jax.numpy as jnp
from jax import lax
from jax.experimental import pallas as pl
from jax.experimental.pallas import tpu as pltpu
from jax.sharding import PartitionSpec as P

C = 256
HEADS = 8
HEAD = 32
WIN = 8
SHIFT = 4
RADIUS = 8
SPAN = 2 * RADIUS + 1
OFFS = SPAN * SPAN
ROWS = 16
COLS = 32
HALO_A = 4
HALO_B = 12
HIGH_A, WIDE_A = 3, 5
HIGH_B, WIDE_B = 5, 7
CELLS = WIN * WIN
SIDE_B = 2 * CELLS
START_A = WIDE_B * SIDE_B
TOTAL = START_A + (WIDE_A + 1) * CELLS
CENTRE = (WIDE_B + WIDE_A) * CELLS

HALF = C // 2
PACKED = 5 * 128
KEYS = 64
GRAM = (ROWS + 2 * RADIUS) * KEYS
FLANK = 2 * WIN * KEYS
LOG2E = 1.4426950408889634
NT = (((1,), (1,)), ((), ()))


def swap(array, axis, step):
    peers = lax.axis_size(axis)
    pairs = [(i, (i ^ 1) if step == 0 else (i - 1 if i % 2 == 0 else i + 1) % peers) for i in range(peers)]
    return lax.ppermute(array, axis, pairs)


def dot(left, right):
    return jnp.dot(left, right, preferred_element_type=jnp.float32)


MID_A = WIDE_B * ROWS * WIN
MID = (WIDE_B + WIDE_A) * ROWS * WIN
SENT_B = HALO_B * WIN
SENT_A = HALO_A * WIN
SENT = WIDE_B * SENT_B + WIDE_A * SENT_A


def pack_cols(ids, a_ref, b_ref, near_ref, far_ref):
    even = ids[1] % 2 == 0
    for r in range(ROWS):
        a, b = a_ref[r].astype(jnp.float32), b_ref[r].astype(jnp.float32)
        first = jnp.concatenate([b[:HALO_B], a[:HALO_A]], axis=0)
        last = jnp.concatenate([b[-HALO_B:], a[-HALO_A:]], axis=0)
        near_ref[r] = jnp.where(even, last, first).astype(jnp.bfloat16)
        far_ref[r] = jnp.where(even, first, last).astype(jnp.bfloat16)


def pack_rows(ids, a_ref, b_ref, near_ref, far_ref, mid, up_ref, down_ref):
    even = ids[1] % 2 == 0
    for r in range(0, ROWS, 2):
        rows = []
        for k in range(2):
            near = near_ref[r + k].astype(jnp.float32)
            far = far_ref[r + k].astype(jnp.float32)
            before, after = jnp.where(even, far, near), jnp.where(even, near, far)
            a = a_ref[r + k].astype(jnp.float32)
            b = b_ref[r + k].astype(jnp.float32)
            b = jnp.concatenate([before[:HALO_B], b, after[:HALO_B]], axis=0)
            a = jnp.concatenate([before[HALO_B:], a, after[HALO_B:]], axis=0)
            rows.append(jnp.concatenate([b, a], axis=0))
        for j in range(WIDE_B + WIDE_A):
            part = slice(WIN * j, WIN * (j + 1))
            mid[(j * ROWS + r) * WIN : (j * ROWS + r + 2) * WIN] = jnp.concatenate(
                [rows[0][part], rows[1][part]], axis=0
            ).astype(jnp.bfloat16)

    def send(out, last):
        for j in range(WIDE_B):
            start = pl.multiple_of(j * ROWS * WIN + last * (ROWS * WIN - SENT_B), 16)
            out[j * SENT_B : (j + 1) * SENT_B] = mid[pl.ds(start, SENT_B)]
        for j in range(WIDE_A):
            start = pl.multiple_of(MID_A + j * ROWS * WIN + last * (ROWS * WIN - SENT_A), 16)
            at = WIDE_B * SENT_B + j * SENT_A
            out[at : at + SENT_A] = mid[pl.ds(start, SENT_A)]

    odd = ids[0] % 2
    send(up_ref, 1 - odd)
    send(down_ref, odd)


def normalise(x, vectors):
    x = x.astype(jnp.float32)
    centred = x - jnp.mean(x, axis=-1, keepdims=True)
    variance = jnp.mean(centred * centred, axis=-1, keepdims=True)
    normed = centred * lax.rsqrt(variance + 1e-05) * vectors[0:1] + vectors[1:2]
    return normed.astype(jnp.bfloat16)


def project(normed, rows, vectors, w_k, w_qv, b_qv, q_s, k_s, v_s):
    k_s[rows] = (dot(normed, w_k[...]) + vectors[4:5]).astype(jnp.bfloat16)
    qv = lax.dot_general(w_qv[...], normed, NT, preferred_element_type=jnp.float32)
    qv = qv + b_qv[:, :1]
    q_s[:, rows] = (qv[:C] * (HEAD**-0.5 * LOG2E)).astype(jnp.bfloat16)
    v_s[:, rows] = qv[C:].astype(jnp.bfloat16)


def attend(tables, q_s, k_s, v_s, mix_s):
    place = lax.broadcasted_iota(jnp.int32, (HALF, C), 0) // HEAD
    which = lax.broadcasted_iota(jnp.int32, (HALF, C), 1) // CELLS
    diagonal = (place == which).astype(jnp.float32).astype(jnp.bfloat16)
    low = lax.broadcasted_iota(jnp.int32, (HEAD, 128), 1) < CELLS
    pairs = [slice(128 * u, 128 * (u + 1)) for u in range(len(tables) // 2)]
    sides = [slice(HALF * side, HALF * (side + 1)) for side in range(2)]
    qs, ks, vs = [], [], []
    for both in pairs:
        queries, values, keys = q_s[:, both], v_s[:, both], k_s[both]
        qs += [queries[:, :CELLS], queries[:, CELLS:]]
        vs += [values[:, :CELLS], values[:, CELLS:]]
        ks += [keys[:CELLS], keys[CELLS:]]
    scores = []
    for q, k in zip(qs, ks):
        for part in sides:
            spread = jnp.concatenate([q[part]] * 4, axis=1) * diagonal
            scores.append(dot(k[:, part], spread))
    weights, scales = [], []
    for w, table in enumerate(tables):
        for side in range(2):
            s = scores[2 * w + side] + table[:, C * side : C * (side + 1)]
            p = jnp.exp2(s - jnp.max(s, axis=0, keepdims=True))
            scales.append(1.0 / jnp.sum(p, axis=0, keepdims=True))
            weights.append(p.astype(jnp.bfloat16))
    results = []
    for w, v in enumerate(vs):
        for side, part in enumerate(sides):
            results.append(dot(v[part], weights[2 * w + side]))
    for u, both in enumerate(pairs):
        mixed = []
        for head in range(HEADS):
            side, at = head // 4, head % 4
            rows = slice(HEAD * at, HEAD * (at + 1))
            cols = slice(128 * (at // 2), 128 * (at // 2 + 1))
            n = 4 * u + side
            a = results[n][rows, cols] * scales[n][:, cols]
            b = results[n + 2][rows, cols] * scales[n + 2][:, cols]
            if at % 2 == 0:
                mixed.append(jnp.where(low, a, pltpu.roll(b, CELLS, 1)))
            else:
                mixed.append(jnp.where(low, pltpu.roll(a, CELLS, 1), b))
        mix_s[both] = jnp.concatenate(mixed, axis=0).T.astype(jnp.bfloat16)


def column(ref, start, high, wide, t):
    return jnp.concatenate(
        [ref[start + (j * high + t) * CELLS : start + (j * high + t + 1) * CELLS] for j in range(wide)],
        axis=0,
    )


def finish(ids, x, total, vectors, mirror, strip, out, at):
    f = x.astype(jnp.float32) + (total + vectors[2:3]).astype(jnp.bfloat16).astype(jnp.float32)
    if strip is None:
        out[at : at + WIN * COLS] = dot(mirror[...], f.astype(jnp.bfloat16)).astype(jnp.bfloat16)
        return
    row_start, col_start = ids[0] * ROWS - HALO_B, ids[1] * COLS - HALO_B
    col_places = col_start + lax.broadcasted_iota(jnp.int32, (KEYS, 1), 0)
    col_inside = (col_places >= 0) & (col_places < ids[3] * COLS)
    blank = jnp.zeros((KEYS - WIDE_B * WIN, C), jnp.float32)
    for r in range(WIN):
        row = jnp.concatenate(
            [f[CELLS * j + WIN * r : CELLS * j + WIN * (r + 1)] for j in range(WIDE_B)] + [blank],
            axis=0,
        )
        place = row_start + strip * WIN + r
        inside = col_inside & (place >= 0) & (place < ids[2] * ROWS)
        out[at + r * KEYS : at + (r + 1) * KEYS] = jnp.where(inside, row, 0.0).astype(jnp.bfloat16)


def centre_windows(ids, mid, vectors, w_k, w_qv, b_qv, bias, outer, q_s, k_s, v_s):
    cells = []
    for j in range(0, WIDE_B + WIDE_A, 4):
        inner = []
        for n in range(j, j + 4):
            at = n * ROWS * WIN
            normed = normalise(mid[at : at + ROWS * WIN], vectors)
            outer[n * CELLS : n * CELLS + SENT_A] = normed[:SENT_A]
            outer[n * CELLS + SENT_A : (n + 1) * CELLS] = normed[-SENT_A:]
            inner.append(normed[SENT_A:-SENT_A])
            cells.append(mid[at + SENT_A : at + SENT_A + CELLS])
        rows = slice(j * CELLS, (j + 4) * CELLS)
        project(jnp.concatenate(inner, axis=0), rows, vectors, w_k, w_qv, b_qv, q_s, k_s, v_s)
    tables = [table_of(ids, bias, j, WIDE_B, 1) for j in range(WIDE_B)]
    tables += [table_of(ids, bias, j, WIDE_A, 0) for j in range(WIDE_A)]
    return cells, tables


def table_of(ids, bias, j, wide, inset, on_row=None):
    index = 0 if on_row is None else on_row.astype(jnp.int32)
    if j == inset:
        index += 2 * (ids[1] == 0).astype(jnp.int32)
    elif j == wide - 1 - inset:
        index += 2 * (ids[1] == ids[3] - 1).astype(jnp.int32)
    return bias.at[index]


def flank_windows(
    ids, top, got, mid, outer, vectors, w_k, w_qv, b_qv, bias, x_s, q_s, k_s, v_s, base
):
    def order(theirs, ours):
        return jnp.where(
            top,
            jnp.concatenate([theirs, ours], axis=0),
            jnp.concatenate([ours, theirs], axis=0),
        )

    def ours(ref, start, size):
        last = start + size - SENT_A
        return jnp.where(top, ref[start : start + SENT_A], ref[last : last + SENT_A])

    normed, start = [], 0
    for j in range(WIDE_B + WIDE_A):
        if j < WIDE_B:
            sent, at, end = j * SENT_B, j * SIDE_B, (j + 1) * SIDE_B
            x = got[sent : sent + SENT_B]
        else:
            n = j - WIDE_B
            sent, at = WIDE_B * SENT_B + n * SENT_A, START_A + n * CELLS
            x, end = got[sent : sent + SENT_A], at + CELLS
        x_s[at:end] = order(x, ours(mid, j * ROWS * WIN, ROWS * WIN))
        normed.append(order(normalise(x, vectors), ours(outer, j * CELLS, CELLS)))
        last = j == WIDE_B + WIDE_A - 1
        if last:
            normed.append(normed[-1])
            end += CELLS
        if last or j in (1, 3, 6):
            part = jnp.concatenate(normed, axis=0)
            rows = slice(base + start, base + end)
            project(part, rows, vectors, w_k, w_qv, b_qv, q_s, k_s, v_s)
            normed, start = [], end

    above = top & (ids[0] == 0)
    below = jnp.logical_not(top) & (ids[0] == ids[2] - 1)
    tables = [
        table_of(ids, bias, j, WIDE_B, 1, edge) for j in range(WIDE_B) for edge in (below, above)
    ]
    tables += [table_of(ids, bias, j, WIDE_A, 0, below | above) for j in range(WIDE_A)]
    return tables + tables[-1:]


def flank_features(ids, top, vectors, w_out, mirror, fb, fa, x_s, mix_s, base):
    strips = [(0, 2, WIDE_B, 0), (0, 2, WIDE_B, 1), (START_A, 1, WIDE_A, 0)]
    sums = [dot(column(mix_s, base + strip[0], *strip[1:]), w_out[...]) for strip in strips]
    for t in range(2):
        strip = jnp.where(top, t, t + 3)
        x = column(x_s, *strips[t])
        finish(ids, x, sums[t], vectors, mirror, strip, fb, t * WIN * KEYS)
    finish(ids, column(x_s, *strips[2]), sums[2], vectors, mirror, None, fa, 0)


def early(
    ids, got, mid, vectors, w_k, w_qv, b_qv, bias, w_out, mirror,
    outer, centre_b, centre_a, near_b, near_a, x_s, q_s, k_s, v_s, mix_s,
):
    top = ids[0] % 2 == 1
    cells, tables = centre_windows(
        ids, mid, vectors, w_k, w_qv, b_qv, bias, outer, q_s, k_s, v_s
    )
    tables += flank_windows(
        ids, top, got, mid, outer, vectors, w_k, w_qv, b_qv, bias, x_s, q_s, k_s, v_s, CENTRE
    )
    attend(tables, q_s, k_s, v_s, mix_s)
    cut = WIDE_B * CELLS
    sum_b, sum_a = dot(mix_s[:cut], w_out[...]), dot(mix_s[cut:CENTRE], w_out[...])
    finish(ids, jnp.concatenate(cells[:WIDE_B], axis=0), sum_b, vectors, mirror, 2, centre_b, 0)
    finish(ids, jnp.concatenate(cells[WIDE_B:], axis=0), sum_a, vectors, mirror, None, centre_a, 0)
    flank_features(ids, top, vectors, w_out, mirror, near_b, near_a, x_s, mix_s, CENTRE)


def body(
    ids,
    got,
    mid,
    outer,
    near_b,
    near_a,
    centre_b,
    centre_a,
    vectors,
    w_k,
    w_qv,
    b_qv,
    bias,
    w_out,
    mirror,
    w_hid,
    w_flow,
    b_flow,
    unmirror,
    out,
    x_s,
    q_s,
    k_s,
    v_s,
    mix_s,
    fb,
    fa,
    g_s,
    e_s,
    stat_s,
):
    even = ids[0] % 2 == 0
    low_b, low_a = (HIGH_B * WIN * KEYS - FLANK), (HIGH_A - 1) * WIN * COLS
    here_b = pl.ds(pl.multiple_of(jnp.where(even, 0, low_b), KEYS), FLANK)
    there_b = pl.ds(pl.multiple_of(jnp.where(even, low_b, 0), KEYS), FLANK)
    here_a = pl.ds(pl.multiple_of(jnp.where(even, 0, low_a), COLS), WIN * COLS)
    there_a = pl.ds(pl.multiple_of(jnp.where(even, low_a, 0), COLS), WIN * COLS)
    fb[there_b] = near_b[...]
    fa[there_a] = near_a[...]
    fb[FLANK : FLANK + WIN * KEYS] = centre_b[...]
    fa[WIN * COLS : 2 * WIN * COLS] = centre_a[...]
    tables = flank_windows(
        ids, even, got, mid, outer, vectors, w_k, w_qv, b_qv, bias, x_s, q_s, k_s, v_s, 0
    )
    attend(tables, q_s, k_s, v_s, mix_s)
    flank_features(
        ids, even, vectors, w_out, mirror, fb.at[here_b], fa.at[here_a], x_s, mix_s, 0
    )

    lane = lax.broadcasted_iota(jnp.int32, (COLS, 128), 1)
    valid = lane % 32 < SPAN
    fore = lane % KEYS < 32
    first = valid & (lane < 32)
    slot = lane // 32
    slot_row = jnp.where(slot == 1, 3, jnp.where(slot == 3, 2, slot // 2)).astype(jnp.float32)
    slot_col = (lane % 32 - RADIUS).astype(jnp.float32)
    second = valid & (lane >= 32)

    for n in range(4):
        top, end = max(0, 8 * n - 16), min(ROWS, 8 * n + 8)
        queries = fa[(HALO_A + top) * COLS : (HALO_A + end) * COLS]
        start = (HALO_B - RADIUS + 8 * n) * KEYS
        keys = fb[start : start + 8 * KEYS]
        g_s[top * COLS : end * COLS, 8 * KEYS * n : 8 * KEYS * (n + 1)] = lax.dot_general(
            queries, keys, NT, preferred_element_type=jnp.float32
        )

    def align(r, n):
        at = 128 * (n + r // 2)
        tile = g_s[COLS * r : COLS * (r + 1), at : at + 128]
        turn = 128 - HALO_A - COLS + 1 - 32 * (n % 2)
        return pltpu.roll(tile, turn, 1, stride=1, stride_axis=0)

    for r in range(ROWS):
        tiles = []
        for n in range(5):
            tile = align(r, 2 * n)
            if n < 4:
                tile = jnp.where(fore, tile, align(r, 2 * n + 1))
            keep = valid
            if r % 2 == 0 and n == 4:
                keep = first
            if r % 2 == 1 and n == 0:
                keep = second
            if n == 4 and r % 2 == 1:
                keep = valid & fore
            tiles.append(jnp.where(keep, tile * (C**-0.5 * LOG2E), -1e30))
        most = tiles[0]
        for tile in tiles[1:]:
            most = jnp.maximum(most, tile)
        most = jnp.max(most, axis=-1, keepdims=True)
        rows = slice((r // 2) * COLS, (r // 2 + 1) * COLS)
        parts = [jnp.exp2(tile - most) for tile in tiles]
        for n, part in enumerate(parts):
            e_s[r % 2, rows, 128 * n : 128 * (n + 1)] = part.astype(jnp.bfloat16)
        whole = parts[0] + parts[1] + parts[2] + parts[3] + parts[4]
        steps = parts[1] + 2.0 * parts[2] + 3.0 * parts[3] + 4.0 * parts[4]
        down = 4.0 * steps + whole * (slot_row - float(r % 2 + RADIUS))
        stats = [
            jnp.sum(x, axis=-1, keepdims=True) for x in (down, whole * slot_col, whole)
        ]
        stat_s[r % 2, rows] = jnp.where(
            lane == 0, stats[0], jnp.where(lane == 1, stats[1], jnp.where(lane == 2, stats[2], 0.0))
        )

    sums = [stat_s[par] for par in range(2)]
    hidden = [dot(e_s[par], w_hid[par * PACKED : (par + 1) * PACKED]) for par in range(2)]
    flows = []
    for par in range(2):
        scale = 1.0 / sums[par][:, 2:3]
        act = jax.nn.gelu(hidden[par] * (scale * OFFS) + vectors[3:4]).astype(jnp.bfloat16)
        flow = sums[par] * scale + dot(act, w_flow[...]) + b_flow[...]
        flows.append(flow.T[:WIN])
    flow = jnp.concatenate(flows, axis=0)
    high = flow.astype(jnp.bfloat16)
    rest = flow - high.astype(jnp.float32)
    mid = rest.astype(jnp.bfloat16)
    tail = (rest - mid.astype(jnp.float32)).astype(jnp.bfloat16)
    flow = dot(high, unmirror[...]) + dot(mid, unmirror[...]) + dot(tail, unmirror[...])
    for r in range(ROWS):
        at = WIN * (r % 2)
        out[:, r, :] = flow[at : at + 2, COLS * (r // 2) : COLS * (r // 2 + 1)]


def prepare(
    gain, shift, w_qkv, b_qkv, rel, w_out, b_out, w_hid, b_hid, w_flow, b_flow,
    vectors, w_k, w_o, w_qv, b_qv, packed, flow_w, flow_b, bias, turn, back,
):
    def iota(shape, dim):
        return lax.broadcasted_iota(jnp.int32, shape, dim)

    def onehot(hit):
        return hit.astype(jnp.float32).astype(jnp.bfloat16)

    lane = iota((2 * PACKED, 1), 0)
    par = (lane >= PACKED).astype(jnp.int32)
    lane = lane - par * PACKED
    slot, dc = lane % 128 // 32, lane % 32
    dr = lane // 128 * 4 + jnp.where(slot == 1, 3, jnp.where(slot == 3, 2, slot // 2)) - par
    inside = (dr >= 0) & (dr < SPAN) & (dc < SPAN)
    place = jnp.where(inside, dr * SPAN + dc, -1)
    pick = onehot(iota((2 * PACKED, OFFS), 1) == place)
    at = iota(turn.shape, 0)
    col = HALO_A + COLS - 1 - at % COLS
    source = col // WIN * CELLS + at // COLS * WIN + col % WIN
    turn[...] = onehot(iota(turn.shape, 1) == source)
    at = iota(back.shape, 0)
    back[...] = onehot(iota(back.shape, 1) == at // COLS * COLS + COLS - 1 - at % COLS)
    side = 2 * WIN - 1
    at = iota((side * side, C), 0)
    spread = onehot(iota(at.shape, 1) == 16 * (at // side + 1) + at % side)
    at = iota((C, 128), 0)
    cell = at % 128 // 16 * WIN + at % 16
    squeeze = onehot((at % 16 < WIN) & (iota(at.shape, 1) == at // 128 * CELLS + cell))

    for n, row in enumerate((gain, shift, b_out, b_hid)):
        vectors[n : n + 1] = row[...]
    vectors[4:5] = b_qkv[:, C : 2 * C]
    vectors[5:8] = jnp.zeros((3, C), jnp.float32)
    w_k[...] = w_qkv[:, C : 2 * C]
    w_o[...] = w_out[...]
    w_qv[:C] = w_qkv[:, :C].T
    w_qv[C:] = w_qkv[:, 2 * C :].T
    b = b_qkv[...]
    b = jnp.concatenate([b[:, :C], b[:, 2 * C :]], axis=1)
    b_qv[...] = jnp.broadcast_to(b, (128, 2 * C)).T
    packed[...] = dot(pick, w_hid[...]).astype(jnp.bfloat16)
    flow_w[...] = jnp.concatenate(
        [w_flow[...].astype(jnp.float32), jnp.zeros((C, 126), jnp.float32)], axis=1
    ).astype(jnp.bfloat16)
    flow_b[...] = jnp.concatenate([b_flow[...], jnp.zeros((1, 126), jnp.float32)], axis=1)

    def exactly(x, onehot):
        high = x.astype(jnp.bfloat16)
        rest = x - high.astype(jnp.float32)
        mid = rest.astype(jnp.bfloat16)
        low = (rest - mid.astype(jnp.float32)).astype(jnp.bfloat16)
        return dot(high, onehot) + dot(mid, onehot) + dot(low, onehot)

    table = exactly(rel[...], spread) * LOG2E
    parts = []
    for head in range(HEADS):
        line = jnp.broadcast_to(table[head : head + 1], (WIN, C))
        rows = []
        for r in range(WIN):
            start = 16 * (WIN - r) - 1
            rows.append(pltpu.roll(line[:, start : start + 128], 120, 1, stride=1, stride_axis=0))
        parts.append(jnp.concatenate(rows, axis=0))
    pairs = [
        exactly(jnp.concatenate(parts[2 * p : 2 * p + 2], axis=1), squeeze)
        for p in range(HEADS // 2)
    ]
    base = jnp.concatenate(pairs, axis=1)
    key = lax.broadcasted_iota(jnp.int32, base.shape, 0)
    query = lax.broadcasted_iota(jnp.int32, base.shape, 1) % CELLS
    rows = (key // WIN < SHIFT) != (query // WIN < SHIFT)
    cols = (key % WIN < SHIFT) != (query % WIN < SHIFT)
    far = base - 100.0 * LOG2E
    bias[0] = base
    bias[1] = jnp.where(rows, far, base)
    bias[2] = jnp.where(cols, far, base)
    bias[3] = jnp.where(rows | cols, far, base)


def shards(
    section_a,
    section_b,
    ln_gain,
    ln_shift,
    w_qkv,
    b_qkv,
    rel_table,
    w_out,
    b_out,
    w_hid,
    b_hid,
    w_flow,
    b_flow,
):
    ids = jnp.stack(
        [
            lax.axis_index("row"),
            lax.axis_index("col"),
            jnp.int32(lax.axis_size("row")),
            jnp.int32(lax.axis_size("col")),
        ]
    )
    scalars = pl.BlockSpec(memory_space=pltpu.SMEM)
    whole = pl.BlockSpec(memory_space=pltpu.VMEM)
    params = pltpu.CompilerParams(vmem_limit_bytes=40 * 1024 * 1024)
    def made(*shape):
        return jax.ShapeDtypeStruct(shape, jnp.bfloat16)

    def made_f32(*shape):
        return jax.ShapeDtypeStruct(shape, jnp.float32)

    made_ready = pl.pallas_call(
        prepare,
        out_shape=(
            made_f32(8, C),
            made(C, C),
            made(C, C),
            made(2 * C, C),
            made_f32(2 * C, 128),
            made(2 * PACKED, C),
            made(C, 128),
            made_f32(1, 128),
            made_f32(4, CELLS, HEADS * CELLS),
            made(WIN * COLS, WIDE_A * CELLS),
            made(C, C),
        ),
        in_specs=[whole] * 11,
        out_specs=(whole,) * 11,
        compiler_params=params,
        cost_estimate=pl.CostEstimate(flops=10**9, bytes_accessed=4 * 10**6, transcendentals=0),
    )(
        ln_gain[None],
        ln_shift[None],
        w_qkv,
        b_qkv[None],
        rel_table,
        w_out,
        b_out[None],
        w_hid,
        b_hid[None],
        w_flow,
        b_flow[None],
    )
    strip = jax.ShapeDtypeStruct((ROWS, HALO_A + HALO_B, C), jnp.bfloat16)
    near, far = pl.pallas_call(
        pack_cols,
        out_shape=(strip, strip),
        in_specs=[scalars, whole, whole],
        out_specs=(whole,) * 2,
        compiler_params=params,
    )(ids, section_a, section_b)
    far = swap(far, "col", 1)
    near = swap(near, "col", 0)
    near, far, made_ready = lax.optimization_barrier((near, far, made_ready))
    vectors, w_k, w_o, w_qv, b_qv, packed, flow_pad, b_flow_pad, bias, turn, back = made_ready
    sent = jax.ShapeDtypeStruct((SENT, C), jnp.bfloat16)
    mid, near, far = pl.pallas_call(
        pack_rows,
        out_shape=(jax.ShapeDtypeStruct((MID, C), jnp.bfloat16), sent, sent),
        in_specs=[scalars] + [whole] * 4,
        out_specs=(whole,) * 3,
        compiler_params=params,
    )(ids, section_a, section_b, near, far)
    near = swap(near, "row", 0)
    far = swap(far, "row", 1)

    tables = (vectors, w_k, w_qv, b_qv, bias, w_o, turn)

    def rooms(cells):
        return [
            pltpu.VMEM((TOTAL, C), jnp.bfloat16),
            pltpu.VMEM((C, cells), jnp.bfloat16),
            pltpu.VMEM((cells, C), jnp.bfloat16),
            pltpu.VMEM((C, cells), jnp.bfloat16),
            pltpu.VMEM((cells, C), jnp.bfloat16),
        ]

    outer, centre_b, centre_a, near_b, near_a = pl.pallas_call(
        early,
        out_shape=(
            made(CENTRE, C),
            made(WIN * KEYS, C),
            made(WIN * COLS, C),
            made(FLANK, C),
            made(WIN * COLS, C),
        ),
        in_specs=[scalars] + [whole] * 9,
        out_specs=(whole,) * 5,
        scratch_shapes=rooms(CENTRE + TOTAL),
        compiler_params=params,
        cost_estimate=pl.CostEstimate(flops=4 * 10**9, bytes_accessed=4 * 10**6, transcendentals=0),
    )(ids, near, mid, *tables)

    return pl.pallas_call(
        body,
        out_shape=jax.ShapeDtypeStruct((2, ROWS, COLS), jnp.float32),
        in_specs=[scalars] + [whole] * 18,
        out_specs=whole,
        scratch_shapes=rooms(TOTAL)
        + [
            pltpu.VMEM((HIGH_B * WIN * KEYS, C), jnp.bfloat16),
            pltpu.VMEM((HIGH_A * WIN * COLS, C), jnp.bfloat16),
            pltpu.VMEM((ROWS * COLS, GRAM), jnp.float32),
            pltpu.VMEM((2, ROWS // 2 * COLS, PACKED), jnp.bfloat16),
            pltpu.VMEM((2, ROWS // 2 * COLS, 128), jnp.float32),
        ],
        compiler_params=params,
    )(
        ids,
        far,
        mid,
        outer,
        near_b,
        near_a,
        centre_b,
        centre_a,
        *tables,
        packed,
        flow_pad,
        b_flow_pad,
        back,
    )


def solution(mesh):
    placed = (P("row", "col", None),) * 2 + (P(),) * 11
    return jax.shard_map(
        shards, mesh=mesh, in_specs=placed, out_specs=P(None, "row", "col"), check_vma=False
    )
```

```python
import jax
import jax.numpy as jnp
from jax import lax
from jax.experimental import pallas as pl
from jax.experimental.pallas import tpu as pltpu
from jax.sharding import PartitionSpec as P

C = 256
HEADS = 8
HEAD = 32
WIN = 8
SHIFT = 4
RADIUS = 8
SPAN = 2 * RADIUS + 1
OFFS = SPAN * SPAN
ROWS = 16
COLS = 32
HALO_A = 4
HALO_B = 12
HIGH_A, WIDE_A = 3, 5
HIGH_B, WIDE_B = 5, 7
CELLS = WIN * WIN
SIDE_B = 2 * CELLS
START_A = WIDE_B * SIDE_B
TOTAL = START_A + (WIDE_A + 1) * CELLS
CENTRE = (WIDE_B + WIDE_A) * CELLS

HALF = C // 2
PACKED = 5 * 128
KEYS = 64
SOON, LATE = 4, 12
FLANK = 2 * WIN * KEYS
LOG2E = 1.4426950408889634
NT = (((1,), (1,)), ((), ()))


def swap(array, axis, step):
    peers = lax.axis_size(axis)
    pairs = [(i, (i ^ 1) if step == 0 else (i - 1 if i % 2 == 0 else i + 1) % peers) for i in range(peers)]
    return lax.ppermute(array, axis, pairs)


def dot(left, right):
    return jnp.dot(left, right, preferred_element_type=jnp.float32)


MID_A = WIDE_B * ROWS * WIN
MID = (WIDE_B + WIDE_A) * ROWS * WIN
SENT_B = HALO_B * WIN
SENT_A = HALO_A * WIN
SENT = WIDE_B * SENT_B + WIDE_A * SENT_A


def pack_cols(ids, a_ref, b_ref, near_ref, far_ref):
    even = ids[1] % 2 == 0
    for r in range(ROWS):
        a, b = a_ref[r].astype(jnp.float32), b_ref[r].astype(jnp.float32)
        first = jnp.concatenate([b[:HALO_B], a[:HALO_A]], axis=0)
        last = jnp.concatenate([b[-HALO_B:], a[-HALO_A:]], axis=0)
        near_ref[r] = jnp.where(even, last, first).astype(jnp.bfloat16)
        far_ref[r] = jnp.where(even, first, last).astype(jnp.bfloat16)


def pack_rows(ids, a_ref, b_ref, near_ref, far_ref, mid, up_ref, down_ref):
    even = ids[1] % 2 == 0
    for r in range(0, ROWS, 2):
        rows = []
        for k in range(2):
            near = near_ref[r + k].astype(jnp.float32)
            far = far_ref[r + k].astype(jnp.float32)
            before, after = jnp.where(even, far, near), jnp.where(even, near, far)
            a = a_ref[r + k].astype(jnp.float32)
            b = b_ref[r + k].astype(jnp.float32)
            b = jnp.concatenate([before[:HALO_B], b, after[:HALO_B]], axis=0)
            a = jnp.concatenate([before[HALO_B:], a, after[HALO_B:]], axis=0)
            rows.append(jnp.concatenate([b, a], axis=0))
        for j in range(WIDE_B + WIDE_A):
            part = slice(WIN * j, WIN * (j + 1))
            mid[(j * ROWS + r) * WIN : (j * ROWS + r + 2) * WIN] = jnp.concatenate(
                [rows[0][part], rows[1][part]], axis=0
            ).astype(jnp.bfloat16)

    def send(out, last):
        for j in range(WIDE_B):
            start = pl.multiple_of(j * ROWS * WIN + last * (ROWS * WIN - SENT_B), 16)
            out[j * SENT_B : (j + 1) * SENT_B] = mid[pl.ds(start, SENT_B)]
        for j in range(WIDE_A):
            start = pl.multiple_of(MID_A + j * ROWS * WIN + last * (ROWS * WIN - SENT_A), 16)
            at = WIDE_B * SENT_B + j * SENT_A
            out[at : at + SENT_A] = mid[pl.ds(start, SENT_A)]

    odd = ids[0] % 2
    send(up_ref, 1 - odd)
    send(down_ref, odd)


def normalise(x, vectors):
    x = x.astype(jnp.float32)
    centred = x - jnp.mean(x, axis=-1, keepdims=True)
    variance = jnp.mean(centred * centred, axis=-1, keepdims=True)
    normed = centred * lax.rsqrt(variance + 1e-05) * vectors[0:1] + vectors[1:2]
    return normed.astype(jnp.bfloat16)


def project(normed, rows, vectors, w_k, w_qv, b_qv, q_s, k_s, v_s):
    k_s[rows] = (dot(normed, w_k[...]) + vectors[4:5]).astype(jnp.bfloat16)
    qv = lax.dot_general(w_qv[...], normed, NT, preferred_element_type=jnp.float32)
    qv = qv + b_qv[:, :1]
    q_s[:, rows] = (qv[:C] * (HEAD**-0.5 * LOG2E)).astype(jnp.bfloat16)
    v_s[:, rows] = qv[C:].astype(jnp.bfloat16)


def attend(tables, q_s, k_s, v_s, mix_s):
    place = lax.broadcasted_iota(jnp.int32, (HALF, C), 0) // HEAD
    which = lax.broadcasted_iota(jnp.int32, (HALF, C), 1) // CELLS
    diagonal = (place == which).astype(jnp.float32).astype(jnp.bfloat16)
    low = lax.broadcasted_iota(jnp.int32, (HEAD, 128), 1) < CELLS
    pairs = [slice(128 * u, 128 * (u + 1)) for u in range(len(tables) // 2)]
    sides = [slice(HALF * side, HALF * (side + 1)) for side in range(2)]
    qs, ks, vs = [], [], []
    for both in pairs:
        queries, values, keys = q_s[:, both], v_s[:, both], k_s[both]
        qs += [queries[:, :CELLS], queries[:, CELLS:]]
        vs += [values[:, :CELLS], values[:, CELLS:]]
        ks += [keys[:CELLS], keys[CELLS:]]
    scores = []
    for q, k in zip(qs, ks):
        for part in sides:
            spread = jnp.concatenate([q[part]] * 4, axis=1) * diagonal
            scores.append(dot(k[:, part], spread))
    weights, scales = [], []
    for w, table in enumerate(tables):
        for side in range(2):
            s = scores[2 * w + side] + table[:, C * side : C * (side + 1)]
            p = jnp.exp2(s - jnp.max(s, axis=0, keepdims=True))
            scales.append(1.0 / jnp.sum(p, axis=0, keepdims=True))
            weights.append(p.astype(jnp.bfloat16))
    results = []
    for w, v in enumerate(vs):
        for side, part in enumerate(sides):
            results.append(dot(v[part], weights[2 * w + side]))
    for u, both in enumerate(pairs):
        mixed = []
        for head in range(HEADS):
            side, at = head // 4, head % 4
            rows = slice(HEAD * at, HEAD * (at + 1))
            cols = slice(128 * (at // 2), 128 * (at // 2 + 1))
            n = 4 * u + side
            a = results[n][rows, cols] * scales[n][:, cols]
            b = results[n + 2][rows, cols] * scales[n + 2][:, cols]
            if at % 2 == 0:
                mixed.append(jnp.where(low, a, pltpu.roll(b, CELLS, 1)))
            else:
                mixed.append(jnp.where(low, pltpu.roll(a, CELLS, 1), b))
        mix_s[both] = jnp.concatenate(mixed, axis=0).T.astype(jnp.bfloat16)


def column(ref, start, high, wide, t):
    return jnp.concatenate(
        [ref[start + (j * high + t) * CELLS : start + (j * high + t + 1) * CELLS] for j in range(wide)],
        axis=0,
    )


def finish(ids, x, total, vectors, mirror, strip, out, at):
    f = x.astype(jnp.float32) + (total + vectors[2:3]).astype(jnp.bfloat16).astype(jnp.float32)
    if strip is None:
        out[at : at + WIN * COLS] = dot(mirror[...], f.astype(jnp.bfloat16)).astype(jnp.bfloat16)
        return
    row_start, col_start = ids[0] * ROWS - HALO_B, ids[1] * COLS - HALO_B
    col_places = col_start + lax.broadcasted_iota(jnp.int32, (KEYS, 1), 0)
    col_inside = (col_places >= 0) & (col_places < ids[3] * COLS)
    blank = jnp.zeros((KEYS - WIDE_B * WIN, C), jnp.float32)
    for r in range(WIN):
        row = jnp.concatenate(
            [f[CELLS * j + WIN * r : CELLS * j + WIN * (r + 1)] for j in range(WIDE_B)] + [blank],
            axis=0,
        )
        place = row_start + strip * WIN + r
        inside = col_inside & (place >= 0) & (place < ids[2] * ROWS)
        out[at + r * KEYS : at + (r + 1) * KEYS] = jnp.where(inside, row, 0.0).astype(jnp.bfloat16)


def centre_windows(ids, mid, vectors, w_k, w_qv, b_qv, bias, outer, q_s, k_s, v_s):
    cells = []
    for j in range(0, WIDE_B + WIDE_A, 4):
        inner = []
        for n in range(j, j + 4):
            at = n * ROWS * WIN
            normed = normalise(mid[at : at + ROWS * WIN], vectors)
            outer[n * CELLS : n * CELLS + SENT_A] = normed[:SENT_A]
            outer[n * CELLS + SENT_A : (n + 1) * CELLS] = normed[-SENT_A:]
            inner.append(normed[SENT_A:-SENT_A])
            cells.append(mid[at + SENT_A : at + SENT_A + CELLS])
        rows = slice(j * CELLS, (j + 4) * CELLS)
        project(jnp.concatenate(inner, axis=0), rows, vectors, w_k, w_qv, b_qv, q_s, k_s, v_s)
    tables = [table_of(ids, bias, j, WIDE_B, 1) for j in range(WIDE_B)]
    tables += [table_of(ids, bias, j, WIDE_A, 0) for j in range(WIDE_A)]
    return cells, tables


def table_of(ids, bias, j, wide, inset, on_row=None):
    index = 0 if on_row is None else on_row.astype(jnp.int32)
    if j == inset:
        index += 2 * (ids[1] == 0).astype(jnp.int32)
    elif j == wide - 1 - inset:
        index += 2 * (ids[1] == ids[3] - 1).astype(jnp.int32)
    return bias.at[index]


def flank_windows(
    ids, top, got, mid, outer, vectors, w_k, w_qv, b_qv, bias, x_s, q_s, k_s, v_s, base
):
    def order(theirs, ours):
        return jnp.where(
            top,
            jnp.concatenate([theirs, ours], axis=0),
            jnp.concatenate([ours, theirs], axis=0),
        )

    def ours(ref, start, size):
        last = start + size - SENT_A
        return jnp.where(top, ref[start : start + SENT_A], ref[last : last + SENT_A])

    normed, start = [], 0
    for j in range(WIDE_B + WIDE_A):
        if j < WIDE_B:
            sent, at, end = j * SENT_B, j * SIDE_B, (j + 1) * SIDE_B
            x = got[sent : sent + SENT_B]
        else:
            n = j - WIDE_B
            sent, at = WIDE_B * SENT_B + n * SENT_A, START_A + n * CELLS
            x, end = got[sent : sent + SENT_A], at + CELLS
        x_s[at:end] = order(x, ours(mid, j * ROWS * WIN, ROWS * WIN))
        normed.append(order(normalise(x, vectors), ours(outer, j * CELLS, CELLS)))
        last = j == WIDE_B + WIDE_A - 1
        if last:
            normed.append(normed[-1])
            end += CELLS
        if last or j in (1, 3, 6):
            part = jnp.concatenate(normed, axis=0)
            rows = slice(base + start, base + end)
            project(part, rows, vectors, w_k, w_qv, b_qv, q_s, k_s, v_s)
            normed, start = [], end

    above = top & (ids[0] == 0)
    below = jnp.logical_not(top) & (ids[0] == ids[2] - 1)
    tables = [
        table_of(ids, bias, j, WIDE_B, 1, edge) for j in range(WIDE_B) for edge in (below, above)
    ]
    tables += [table_of(ids, bias, j, WIDE_A, 0, below | above) for j in range(WIDE_A)]
    return tables + tables[-1:]


def flank_features(ids, top, vectors, w_out, mirror, fb, fa, x_s, mix_s, base):
    strips = [(0, 2, WIDE_B, 0), (0, 2, WIDE_B, 1), (START_A, 1, WIDE_A, 0)]
    sums = [dot(column(mix_s, base + strip[0], *strip[1:]), w_out[...]) for strip in strips]
    for t in range(2):
        strip = jnp.where(top, t, t + 3)
        x = column(x_s, *strips[t])
        finish(ids, x, sums[t], vectors, mirror, strip, fb, t * WIN * KEYS)
    finish(ids, column(x_s, *strips[2]), sums[2], vectors, mirror, None, fa, 0)


def correlate(
    count, queries, keys, vectors, w_hid, w_flow, b_flow, unmirror, g_s, e_s, stat_s
):
    lane = lax.broadcasted_iota(jnp.int32, (COLS, 128), 1)
    valid = lane % 32 < SPAN
    fore = lane % KEYS < 32
    first = valid & (lane < 32)
    slot = lane // 32
    slot_row = jnp.where(slot == 1, 3, jnp.where(slot == 3, 2, slot // 2)).astype(jnp.float32)
    slot_col = (lane % 32 - RADIUS).astype(jnp.float32)
    second = valid & (lane >= 32)

    for start in range(0, count + 2 * RADIUS, 8):
        stop = min(count + 2 * RADIUS, start + 8)
        top, end = max(0, start - 2 * RADIUS), min(count, stop)
        g_s[top * COLS : end * COLS, start * KEYS : stop * KEYS] = lax.dot_general(
            queries[top * COLS : end * COLS],
            keys[start * KEYS : stop * KEYS],
            NT,
            preferred_element_type=jnp.float32,
        )

    def align(r, n):
        at = 128 * (n + r // 2)
        tile = g_s[COLS * r : COLS * (r + 1), at : at + 128]
        turn = 128 - HALO_A - COLS + 1 - 32 * (n % 2)
        return pltpu.roll(tile, turn, 1, stride=1, stride_axis=0)

    for r in range(count):
        tiles = []
        for n in range(5):
            tile = align(r, 2 * n)
            if n < 4:
                tile = jnp.where(fore, tile, align(r, 2 * n + 1))
            keep = valid
            if r % 2 == 0 and n == 4:
                keep = first
            if r % 2 == 1 and n == 0:
                keep = second
            if n == 4 and r % 2 == 1:
                keep = valid & fore
            tiles.append(jnp.where(keep, tile * (C**-0.5 * LOG2E), -1e30))
        most = tiles[0]
        for tile in tiles[1:]:
            most = jnp.maximum(most, tile)
        most = jnp.max(most, axis=-1, keepdims=True)
        rows = slice((r // 2) * COLS, (r // 2 + 1) * COLS)
        parts = [jnp.exp2(tile - most) for tile in tiles]
        for n, part in enumerate(parts):
            e_s[r % 2, rows, 128 * n : 128 * (n + 1)] = part.astype(jnp.bfloat16)
        whole = parts[0] + parts[1] + parts[2] + parts[3] + parts[4]
        steps = parts[1] + 2.0 * parts[2] + 3.0 * parts[3] + 4.0 * parts[4]
        down = 4.0 * steps + whole * (slot_row - float(r % 2 + RADIUS))
        stats = [
            jnp.sum(x, axis=-1, keepdims=True) for x in (down, whole * slot_col, whole)
        ]
        stat_s[r % 2, rows] = jnp.where(
            lane == 0, stats[0], jnp.where(lane == 1, stats[1], jnp.where(lane == 2, stats[2], 0.0))
        )

    sums = [stat_s[par] for par in range(2)]
    hidden = [dot(e_s[par], w_hid[par * PACKED : (par + 1) * PACKED]) for par in range(2)]
    flows = []
    for par in range(2):
        scale = 1.0 / sums[par][:, 2:3]
        act = jax.nn.gelu(hidden[par] * (scale * OFFS) + vectors[3:4]).astype(jnp.bfloat16)
        flow = sums[par] * scale + dot(act, w_flow[...]) + b_flow[...]
        size = count // 2 * COLS
        more = -size % 128
        if more:
            flow = jnp.concatenate([flow, jnp.zeros((more, 128), jnp.float32)], axis=0)
        flows.append(flow.T[:WIN])
    flow = jnp.concatenate(flows, axis=0)
    high = flow.astype(jnp.bfloat16)
    rest = flow - high.astype(jnp.float32)
    mid = rest.astype(jnp.bfloat16)
    tail = (rest - mid.astype(jnp.float32)).astype(jnp.bfloat16)
    turned = unmirror[: flow.shape[1], : flow.shape[1]]
    flow = dot(high, turned) + dot(mid, turned) + dot(tail, turned)
    return [
        flow[WIN * (r % 2) : WIN * (r % 2) + 2, COLS * (r // 2) : COLS * (r // 2 + 1)]
        for r in range(count)
    ]


def early(
    ids, got, mid, vectors, w_k, w_qv, b_qv, bias, w_out, mirror, w_hid, w_flow, b_flow, unmirror,
    outer, centre_b, centre_a, near_b, near_a, ready,
    x_s, q_s, k_s, v_s, mix_s, fb, g_s, e_s, stat_s,
):
    top = ids[0] % 2 == 1
    cells, tables = centre_windows(
        ids, mid, vectors, w_k, w_qv, b_qv, bias, outer, q_s, k_s, v_s
    )
    tables += flank_windows(
        ids, top, got, mid, outer, vectors, w_k, w_qv, b_qv, bias, x_s, q_s, k_s, v_s, CENTRE
    )
    attend(tables, q_s, k_s, v_s, mix_s)
    cut = WIDE_B * CELLS
    sum_b, sum_a = dot(mix_s[:cut], w_out[...]), dot(mix_s[cut:CENTRE], w_out[...])
    finish(ids, jnp.concatenate(cells[:WIDE_B], axis=0), sum_b, vectors, mirror, 2, centre_b, 0)
    finish(ids, jnp.concatenate(cells[WIDE_B:], axis=0), sum_a, vectors, mirror, None, centre_a, 0)
    flank_features(ids, top, vectors, w_out, mirror, near_b, near_a, x_s, mix_s, CENTRE)
    strip = WIN * KEYS
    fb[pl.ds(pl.multiple_of(jnp.where(top, FLANK, 0), strip), strip)] = centre_b[...]
    fb[pl.ds(pl.multiple_of(jnp.where(top, 0, strip), strip), FLANK)] = near_b[...]
    skip = jnp.where(top, HALO_A, 0)
    queries = near_a.at[pl.ds(pl.multiple_of(skip * COLS, COLS), SOON * COLS)]
    reach = (SOON + 2 * RADIUS) * KEYS
    keys = fb.at[pl.ds(pl.multiple_of(skip * KEYS, KEYS), reach)]
    flows = correlate(
        SOON, queries, keys, vectors, w_hid, w_flow, b_flow, unmirror, g_s, e_s, stat_s
    )
    for r, flow in enumerate(flows):
        ready[:, r, :] = flow


def body(
    ids,
    got,
    mid,
    outer,
    near_b,
    near_a,
    centre_b,
    centre_a,
    ready,
    vectors,
    w_k,
    w_qv,
    b_qv,
    bias,
    w_out,
    mirror,
    w_hid,
    w_flow,
    b_flow,
    unmirror,
    out,
    x_s,
    q_s,
    k_s,
    v_s,
    mix_s,
    fb,
    fa,
    g_s,
    e_s,
    stat_s,
):
    even = ids[0] % 2 == 0
    low_b, low_a = (HIGH_B * WIN * KEYS - FLANK), (HIGH_A - 1) * WIN * COLS
    here_b = pl.ds(pl.multiple_of(jnp.where(even, 0, low_b), KEYS), FLANK)
    there_b = pl.ds(pl.multiple_of(jnp.where(even, low_b, 0), KEYS), FLANK)
    here_a = pl.ds(pl.multiple_of(jnp.where(even, 0, low_a), COLS), WIN * COLS)
    there_a = pl.ds(pl.multiple_of(jnp.where(even, low_a, 0), COLS), WIN * COLS)
    fb[there_b] = near_b[...]
    fa[there_a] = near_a[...]
    fb[FLANK : FLANK + WIN * KEYS] = centre_b[...]
    fa[WIN * COLS : 2 * WIN * COLS] = centre_a[...]
    tables = flank_windows(
        ids, even, got, mid, outer, vectors, w_k, w_qv, b_qv, bias, x_s, q_s, k_s, v_s, 0
    )
    attend(tables, q_s, k_s, v_s, mix_s)
    flank_features(
        ids, even, vectors, w_out, mirror, fb.at[here_b], fa.at[here_a], x_s, mix_s, 0
    )

    base = jnp.where(even, 0, SOON)
    rest = jnp.where(even, LATE, 0)
    queries = fa.at[pl.ds(pl.multiple_of((HALO_A + base) * COLS, COLS), LATE * COLS)]
    reach = (LATE + 2 * RADIUS) * KEYS
    keys = fb.at[pl.ds(pl.multiple_of((HALO_B - RADIUS + base) * KEYS, KEYS), reach)]
    flows = correlate(
        LATE, queries, keys, vectors, w_hid, w_flow, b_flow, unmirror, g_s, e_s, stat_s
    )
    for r, flow in enumerate(flows):
        out[:, pl.ds(base + r, 1), :] = flow[:, None, :]
    for r in range(SOON):
        out[:, pl.ds(rest + r, 1), :] = ready[:, r : r + 1, :]


def prepare(
    gain, shift, w_qkv, b_qkv, rel, w_out, b_out, w_hid, b_hid, w_flow, b_flow,
    vectors, w_k, w_o, w_qv, b_qv, packed, flow_w, flow_b, bias, turn, back,
):
    def iota(shape, dim):
        return lax.broadcasted_iota(jnp.int32, shape, dim)

    def onehot(hit):
        return hit.astype(jnp.float32).astype(jnp.bfloat16)

    lane = iota((2 * PACKED, 1), 0)
    par = (lane >= PACKED).astype(jnp.int32)
    lane = lane - par * PACKED
    slot, dc = lane % 128 // 32, lane % 32
    dr = lane // 128 * 4 + jnp.where(slot == 1, 3, jnp.where(slot == 3, 2, slot // 2)) - par
    inside = (dr >= 0) & (dr < SPAN) & (dc < SPAN)
    place = jnp.where(inside, dr * SPAN + dc, -1)
    pick = onehot(iota((2 * PACKED, OFFS), 1) == place)
    at = iota(turn.shape, 0)
    col = HALO_A + COLS - 1 - at % COLS
    source = col // WIN * CELLS + at // COLS * WIN + col % WIN
    turn[...] = onehot(iota(turn.shape, 1) == source)
    at = iota(back.shape, 0)
    back[...] = onehot(iota(back.shape, 1) == at // COLS * COLS + COLS - 1 - at % COLS)
    side = 2 * WIN - 1
    at = iota((side * side, C), 0)
    spread = onehot(iota(at.shape, 1) == 16 * (at // side + 1) + at % side)
    at = iota((C, 128), 0)
    cell = at % 128 // 16 * WIN + at % 16
    squeeze = onehot((at % 16 < WIN) & (iota(at.shape, 1) == at // 128 * CELLS + cell))

    for n, row in enumerate((gain, shift, b_out, b_hid)):
        vectors[n : n + 1] = row[...]
    vectors[4:5] = b_qkv[:, C : 2 * C]
    vectors[5:8] = jnp.zeros((3, C), jnp.float32)
    w_k[...] = w_qkv[:, C : 2 * C]
    w_o[...] = w_out[...]
    w_qv[:C] = w_qkv[:, :C].T
    w_qv[C:] = w_qkv[:, 2 * C :].T
    b = b_qkv[...]
    b = jnp.concatenate([b[:, :C], b[:, 2 * C :]], axis=1)
    b_qv[...] = jnp.broadcast_to(b, (128, 2 * C)).T
    packed[...] = dot(pick, w_hid[...]).astype(jnp.bfloat16)
    flow_w[...] = jnp.concatenate(
        [w_flow[...].astype(jnp.float32), jnp.zeros((C, 126), jnp.float32)], axis=1
    ).astype(jnp.bfloat16)
    flow_b[...] = jnp.concatenate([b_flow[...], jnp.zeros((1, 126), jnp.float32)], axis=1)

    def exactly(x, onehot):
        high = x.astype(jnp.bfloat16)
        rest = x - high.astype(jnp.float32)
        mid = rest.astype(jnp.bfloat16)
        low = (rest - mid.astype(jnp.float32)).astype(jnp.bfloat16)
        return dot(high, onehot) + dot(mid, onehot) + dot(low, onehot)

    table = exactly(rel[...], spread) * LOG2E
    parts = []
    for head in range(HEADS):
        line = jnp.broadcast_to(table[head : head + 1], (WIN, C))
        rows = []
        for r in range(WIN):
            start = 16 * (WIN - r) - 1
            rows.append(pltpu.roll(line[:, start : start + 128], 120, 1, stride=1, stride_axis=0))
        parts.append(jnp.concatenate(rows, axis=0))
    pairs = [
        exactly(jnp.concatenate(parts[2 * p : 2 * p + 2], axis=1), squeeze)
        for p in range(HEADS // 2)
    ]
    base = jnp.concatenate(pairs, axis=1)
    key = lax.broadcasted_iota(jnp.int32, base.shape, 0)
    query = lax.broadcasted_iota(jnp.int32, base.shape, 1) % CELLS
    rows = (key // WIN < SHIFT) != (query // WIN < SHIFT)
    cols = (key % WIN < SHIFT) != (query % WIN < SHIFT)
    far = base - 100.0 * LOG2E
    bias[0] = base
    bias[1] = jnp.where(rows, far, base)
    bias[2] = jnp.where(cols, far, base)
    bias[3] = jnp.where(rows | cols, far, base)


def shards(
    section_a,
    section_b,
    ln_gain,
    ln_shift,
    w_qkv,
    b_qkv,
    rel_table,
    w_out,
    b_out,
    w_hid,
    b_hid,
    w_flow,
    b_flow,
):
    ids = jnp.stack(
        [
            lax.axis_index("row"),
            lax.axis_index("col"),
            jnp.int32(lax.axis_size("row")),
            jnp.int32(lax.axis_size("col")),
        ]
    )
    scalars = pl.BlockSpec(memory_space=pltpu.SMEM)
    whole = pl.BlockSpec(memory_space=pltpu.VMEM)
    params = pltpu.CompilerParams(vmem_limit_bytes=40 * 1024 * 1024)
    def made(*shape):
        return jax.ShapeDtypeStruct(shape, jnp.bfloat16)

    def made_f32(*shape):
        return jax.ShapeDtypeStruct(shape, jnp.float32)

    made_ready = pl.pallas_call(
        prepare,
        out_shape=(
            made_f32(8, C),
            made(C, C),
            made(C, C),
            made(2 * C, C),
            made_f32(2 * C, 128),
            made(2 * PACKED, C),
            made(C, 128),
            made_f32(1, 128),
            made_f32(4, CELLS, HEADS * CELLS),
            made(WIN * COLS, WIDE_A * CELLS),
            made(C, C),
        ),
        in_specs=[whole] * 11,
        out_specs=(whole,) * 11,
        compiler_params=params,
        cost_estimate=pl.CostEstimate(flops=10**9, bytes_accessed=4 * 10**6, transcendentals=0),
    )(
        ln_gain[None],
        ln_shift[None],
        w_qkv,
        b_qkv[None],
        rel_table,
        w_out,
        b_out[None],
        w_hid,
        b_hid[None],
        w_flow,
        b_flow[None],
    )
    strip = jax.ShapeDtypeStruct((ROWS, HALO_A + HALO_B, C), jnp.bfloat16)
    near, far = pl.pallas_call(
        pack_cols,
        out_shape=(strip, strip),
        in_specs=[scalars, whole, whole],
        out_specs=(whole,) * 2,
        compiler_params=params,
    )(ids, section_a, section_b)
    far = swap(far, "col", 1)
    near = swap(near, "col", 0)
    near, far, made_ready = lax.optimization_barrier((near, far, made_ready))
    vectors, w_k, w_o, w_qv, b_qv, packed, flow_pad, b_flow_pad, bias, turn, back = made_ready
    sent = jax.ShapeDtypeStruct((SENT, C), jnp.bfloat16)
    mid, near, far = pl.pallas_call(
        pack_rows,
        out_shape=(jax.ShapeDtypeStruct((MID, C), jnp.bfloat16), sent, sent),
        in_specs=[scalars] + [whole] * 4,
        out_specs=(whole,) * 3,
        compiler_params=params,
    )(ids, section_a, section_b, near, far)
    near = swap(near, "row", 0)
    far = swap(far, "row", 1)

    tables = (vectors, w_k, w_qv, b_qv, bias, w_o, turn)

    def rooms(cells):
        return [
            pltpu.VMEM((TOTAL, C), jnp.bfloat16),
            pltpu.VMEM((C, cells), jnp.bfloat16),
            pltpu.VMEM((cells, C), jnp.bfloat16),
            pltpu.VMEM((C, cells), jnp.bfloat16),
            pltpu.VMEM((cells, C), jnp.bfloat16),
        ]

    def tiles(count):
        return [
            pltpu.VMEM((count * COLS, (count + 2 * RADIUS) * KEYS), jnp.float32),
            pltpu.VMEM((2, count // 2 * COLS, PACKED), jnp.bfloat16),
            pltpu.VMEM((2, count // 2 * COLS, 128), jnp.float32),
        ]

    outer, centre_b, centre_a, near_b, near_a, ready = pl.pallas_call(
        early,
        out_shape=(
            made(CENTRE, C),
            made(WIN * KEYS, C),
            made(WIN * COLS, C),
            made(FLANK, C),
            made(WIN * COLS, C),
            made_f32(2, SOON, COLS),
        ),
        in_specs=[scalars] + [whole] * 13,
        out_specs=(whole,) * 6,
        scratch_shapes=rooms(CENTRE + TOTAL)
        + [pltpu.VMEM((3 * WIN * KEYS, C), jnp.bfloat16)]
        + tiles(SOON),
        compiler_params=params,
        cost_estimate=pl.CostEstimate(flops=4 * 10**9, bytes_accessed=4 * 10**6, transcendentals=0),
    )(ids, near, mid, *tables, packed, flow_pad, b_flow_pad, back)

    return pl.pallas_call(
        body,
        out_shape=jax.ShapeDtypeStruct((2, ROWS, COLS), jnp.float32),
        in_specs=[scalars] + [whole] * 19,
        out_specs=whole,
        scratch_shapes=rooms(TOTAL)
        + [
            pltpu.VMEM((HIGH_B * WIN * KEYS, C), jnp.bfloat16),
            pltpu.VMEM((HIGH_A * WIN * COLS, C), jnp.bfloat16),
        ]
        + tiles(LATE),
        compiler_params=params,
    )(
        ids,
        far,
        mid,
        outer,
        near_b,
        near_a,
        centre_b,
        centre_a,
        ready,
        *tables,
        packed,
        flow_pad,
        b_flow_pad,
        back,
    )


def solution(mesh):
    placed = (P("row", "col", None),) * 2 + (P(),) * 11
    return jax.shard_map(
        shards, mesh=mesh, in_specs=placed, out_specs=P(None, "row", "col"), check_vma=False
    )
```
